128 devices in a mesh: ctx: 4 (over x_lo, core), exp: 32 (over z, x_hi, y).
Axes of the slice: x: 4 (x_hi: 2, x_lo: 2; x = x_hi * 2 + x_lo), y: 4, z: 4, core: 2. Of those that a mesh axis runs over, the one named last changes fastest.
Arguments:
- queries: bfloat16 [16384, 4096], P(('ctx', 'exp')), may hold values from -6 to 6
- fresh_keys: bfloat16 [16384, 256], P(('ctx', 'exp')), may hold values from -6 to 6
- fresh_values: bfloat16 [16384, 256], P(('ctx', 'exp')), may hold values from -6 to 6
- stored_keys: bfloat16 [8192, 256], P('ctx'), may hold values from -6 to 6
- stored_values: bfloat16 [8192, 256], P('ctx'), may hold values from -6 to 6
- column_blocks: int32 [2, 2], replicated, may hold values from 0 to 127, as said below
- diagonal_offsets: int32 [2, 8], replicated, may hold values from 257 to 384
- residual: bfloat16 [16384, 4096], P(('ctx', 'exp')), may hold values from -3 to 3
- norm_gain: float32 [4096], replicated, may hold values from 0.1 to 1.9
- routes: int32 [16384, 8], P(('ctx', 'exp')), may hold values from 0 to 127, all different within a row; in each aligned block of 128 rows (0 to 127, 128 to 255, ...) at most 10 rows name the same one
- gate_weights: float32 [16384, 8], P(('ctx', 'exp')), may hold values from 0.05 to 1
- w_gate: bfloat16 [128, 4096, 768], P(('ctx', 'exp')), may hold values from -0.09375 to 0.09375
- w_up: bfloat16 [128, 4096, 768], P(('ctx', 'exp')), may hold values from -0.09375 to 0.09375
- w_down: bfloat16 [128, 768, 4096], P(('ctx', 'exp')), may hold values from -0.21875 to 0.21875
Outputs:
- mixed: bfloat16 [16384, 4096], P(('ctx', 'exp'))
The draws below stay inside these ranges and needn't reach their ends.
Inputs may be any that keep to these rules, and one draw needn't show every extreme that they name: `column_blocks`: the vertical blocks of one key-value head differ; the first key-value head reads the last block and the last key-value head reads block 0. `routes`: the 8 experts of a token differ. In each aligned block of 128 tokens (the tokens of one device) no expert is named more than 10 times, a bound that some block reaches.
All inputs are finite; a program needn't handle non-finite values.
Results may differ from the reference program's by a relative error of at most 0.014.
Values may be sent and summed in bfloat16 or wider, within the bound.
A program may use at most 192 MiB of HBM per device.

```python
import math
import jax
import jax.numpy as jnp
import numpy as np
from jax import lax

HEAD_SIZE = 128
QUERY_HEADS = 32
KEY_VALUE_HEADS = 2
D = 4096
FF = 768
TOP = 8
PATTERN_BLOCK = 64
VERTICAL_COUNT = 2
SLASH_COUNT = 8
TOK_DEV = 128
TOKEN_COUNT = 16384
CACHE_LENGTH = 8192
EXPERTS = 128
CAP = 10
N_CTX = 4
N_EXP = 32


def draw_queries(key, part):
    key = jax.random.fold_in(key, 11)
    value_matrix = jnp.clip(jax.random.normal(key, (TOKEN_COUNT, QUERY_HEADS, HEAD_SIZE), jnp.float32), -6.0, 6.0)
    return value_matrix.reshape(TOKEN_COUNT, QUERY_HEADS * HEAD_SIZE).astype(jnp.bfloat16)


def draw_fresh_keys(key, part):
    key = jax.random.fold_in(key, 12)
    value_matrix = jnp.clip(jax.random.normal(key, (TOKEN_COUNT, KEY_VALUE_HEADS, HEAD_SIZE), jnp.float32), -6.0, 6.0)
    return value_matrix.reshape(TOKEN_COUNT, KEY_VALUE_HEADS * HEAD_SIZE).astype(jnp.bfloat16)


def draw_column_blocks(key, part):
    key = jax.random.fold_in(key, 21)
    block_total = CACHE_LENGTH // PATTERN_BLOCK
    head_keys = jax.random.split(key, KEY_VALUE_HEADS)
    chosen = jax.vmap(lambda one_key: jax.random.permutation(one_key, block_total - 2)[:VERTICAL_COUNT])(head_keys) + 1
    chosen = chosen.at[0, 0].set(block_total - 1)
    chosen = chosen.at[KEY_VALUE_HEADS - 1, VERTICAL_COUNT - 1].set(0)
    return chosen.astype(jnp.int32)


def touch_ends(result, own_key, low, high):
    longest = result.shape.index(max(result.shape))
    spots = []
    for shift in (0, 1):
        where = [jax.random.randint(jax.random.fold_in(own_key, axis), (), 0, length) for axis, length in enumerate(result.shape)]
        where[longest] = (where[longest] + shift) % result.shape[longest]
        spots.append(tuple(where))
    return result.at[spots[0]].set(low).at[spots[1]].set(high)


def levels(own_key, dims, shards, smallest, high):
    def one(axis_at, blocks):
        heights = jax.random.uniform(jax.random.fold_in(jax.random.fold_in(own_key, 6), axis_at), (blocks,), jnp.float32, smallest / len(shards), high / len(shards))
        return jnp.repeat(jnp.exp(heights), dims[axis_at] // blocks).reshape((-1,) + (1,) * (len(dims) - axis_at - 1))

    level = one(*shards[0])
    for cut in shards[1:]:
        level = level * one(*cut)
    return level


def assign_block(own_key, own, number, rows, amount, top, bound, slope):
    ranking = jax.random.permutation(own_key, amount)
    crowded, ordinary = shares(amount, rows * top, bound, slope, True), shares(amount, rows * top, bound, slope, False)
    places = jnp.arange(amount)

    def named(sizes, turn):
        used = int((sizes > 0).sum())
        fixed = max(1, used // 4)
        moved = fixed + (places - fixed + turn * (used - fixed)) % max(1, amount - fixed)
        return jnp.zeros((amount,), jnp.int32).at[ranking[jnp.where(places < fixed, places, moved)]].set(jnp.asarray(sizes, jnp.int32))

    sizes = jnp.where(number % 4 == 0, named(crowded, number // 4), named(ordinary, number - number // 4 - 1))
    mixed = jax.random.permutation(jax.random.fold_in(own, 3), amount)
    source_of, taker = mixed[0:amount // 2 * 2:2], mixed[1:amount // 2 * 2:2]
    room = jnp.minimum(sizes[source_of] - 1, bound - sizes[taker]) // 2
    room = jnp.where((source_of == ranking[0]) | (taker == ranking[0]) | (sizes[taker] == 0), 0, jnp.maximum(room, 0))
    moved = jax.random.randint(jax.random.fold_in(own, 4), (amount // 2,), 0, 1 << 20) % (room + 1)
    sizes = sizes.at[source_of].add(-moved).at[taker].add(moved)
    items = jnp.searchsorted(jnp.cumsum(sizes), jnp.arange(rows * top), side="right").astype(jnp.int32)
    table = items.reshape(top, rows).T
    table = table[jax.random.permutation(jax.random.fold_in(own, 1), rows)]
    turn = jax.random.randint(jax.random.fold_in(own, 2), (rows, 1), 0, top)
    return jnp.take_along_axis(table, (jnp.arange(top)[None, :] + turn) % top, axis=1)


def shares(number_of, total, limit, lean, full):
    weights = [(1 << 20) // math.isqrt(grade ** lean) + 1 for grade in range(1, number_of + 1)]
    largest = limit if full else min(limit, max(-(-total // number_of), total * weights[0] // sum(weights)))
    least = 1 if total - largest >= number_of - 1 else 0
    holding, rest = [largest] + [least] * (number_of - 1), total - largest - least * (number_of - 1)
    while rest > 0:
        movable = [i for i in range(1, number_of) if holding[i] < largest] or [i for i in range(1, number_of) if holding[i] < limit]
        pool, left = sum([weights[i] for i in movable]), rest
        for i in movable:
            extra = min(limit - holding[i], max(1, left * weights[i] // pool), rest)
            holding[i] = holding[i] + extra
            rest = rest - extra
    return np.array(holding)


def scatter_about(own_key, extent, deviation, bound, cuts=(), held_as=jnp.bfloat16):
    factor_of = levels(own_key, extent, cuts, -0.22, 0.18) if cuts else 1.0
    values = jax.random.normal(own_key, extent, jnp.float32) * deviation * factor_of
    return jnp.minimum(jnp.maximum(values, -bound), bound).astype(held_as)


def setup_inputs(seed: int = 0) -> dict:
    arg_keys = jax.random.split(jax.random.key(seed), 15)
    queries = draw_queries(jax.random.fold_in(arg_keys[14], 71), 0)
    fresh_keys = draw_fresh_keys(jax.random.fold_in(arg_keys[14], 71), 0)
    fresh_values = scatter_about(arg_keys[2], (TOKEN_COUNT, KEY_VALUE_HEADS * HEAD_SIZE), 1.0, 6.0, ((0, 128),))
    stored_keys = scatter_about(arg_keys[3], (CACHE_LENGTH, KEY_VALUE_HEADS * HEAD_SIZE), 1.0, 6.0, ((0, 4),))
    stored_values = scatter_about(arg_keys[4], (CACHE_LENGTH, KEY_VALUE_HEADS * HEAD_SIZE), 1.0, 6.0, ((0, 4),))
    column_blocks = draw_column_blocks(jax.random.fold_in(arg_keys[14], 71), 0)
    diagonal_offsets = touch_ends(jax.random.randint(arg_keys[6], (KEY_VALUE_HEADS, SLASH_COUNT), TOKEN_COUNT // PATTERN_BLOCK + 1, (CACHE_LENGTH + TOKEN_COUNT) // PATTERN_BLOCK + 1), jax.random.fold_in(arg_keys[6], 1), TOKEN_COUNT // PATTERN_BLOCK + 1, ((CACHE_LENGTH + TOKEN_COUNT) // PATTERN_BLOCK + 1) - 1).astype(jnp.int32)
    residual = scatter_about(arg_keys[7], (TOKEN_COUNT, D), 0.5, 3.0, ((0, 128),))
    norm_gain = jnp.clip(1.0 + 0.18 * jax.random.normal(arg_keys[8], (D,), jnp.float32), 0.1, 1.9)
    routes_keys = jax.random.split(jax.random.fold_in(arg_keys[9], 1), TOKEN_COUNT // TOK_DEV)
    routes_turns = jax.random.permutation(jax.random.fold_in(arg_keys[9], 3), TOKEN_COUNT // TOK_DEV)
    routes = jax.vmap(lambda own, number: assign_block(jax.random.fold_in(arg_keys[9], 2), own, number, TOK_DEV, EXPERTS, TOP, CAP, 2))(routes_keys, routes_turns).reshape((TOKEN_COUNT, TOP))
    gate_weights = jnp.clip(0.05 + 0.95 * jax.random.uniform(arg_keys[10], (TOKEN_COUNT, TOP), jnp.float32) ** levels(arg_keys[10], (TOKEN_COUNT, TOP), ((0, 128),), -0.2, 0.2), 0.05, 1.0)
    w_gate = scatter_about(arg_keys[11], (EXPERTS, D, FF), D ** -0.5, 0.09375, ((0, 128),))
    w_up = scatter_about(arg_keys[12], (EXPERTS, D, FF), D ** -0.5, 0.09375, ((0, 128),))
    w_down = scatter_about(arg_keys[13], (EXPERTS, FF, D), FF ** -0.5, 0.21875, ((0, 128),))
    return dict(queries=queries, fresh_keys=fresh_keys, fresh_values=fresh_values, stored_keys=stored_keys, stored_values=stored_values, column_blocks=column_blocks, diagonal_offsets=diagonal_offsets, residual=residual, norm_gain=norm_gain, routes=routes, gate_weights=gate_weights, w_gate=w_gate, w_up=w_up, w_down=w_down)


def candidates(query_block, column_blocks, diagonal_offsets, block_total):
    count = query_block.shape[0]
    heads = column_blocks.shape[0]
    vertical = jnp.broadcast_to(column_blocks[None, :, :], (count, heads, column_blocks.shape[1])).astype(jnp.int32)
    slash = (query_block[:, None, None] - diagonal_offsets[None, :, :]).astype(jnp.int32)
    listed = jnp.concatenate([vertical, slash], axis=2).astype(jnp.int32)
    width = listed.shape[2]
    inside = (listed >= 0) & (listed < block_total)
    earlier = jnp.arange(width, dtype=jnp.int32)[None, :] < jnp.arange(width, dtype=jnp.int32)[:, None]
    repeated = jnp.any((listed[:, :, :, None] == listed[:, :, None, :]) & earlier[None, None, :, :], axis=-1)
    return (listed, inside & jnp.logical_not(repeated))

def reference(queries, fresh_keys, fresh_values, stored_keys, stored_values, column_blocks, diagonal_offsets, residual, norm_gain, routes, gate_weights, w_gate, w_up, w_down):
    head_groups = QUERY_HEADS // KEY_VALUE_HEADS
    score_scale = 1.0 / HEAD_SIZE ** 0.5
    rows_per_block = min(512, TOKEN_COUNT)
    count_of_queries = rows_per_block // PATTERN_BLOCK
    block_total = CACHE_LENGTH // PATTERN_BLOCK
    key_head_rows = stored_keys.astype(jnp.float32).reshape(CACHE_LENGTH, KEY_VALUE_HEADS, HEAD_SIZE)
    value_head_rows = stored_values.astype(jnp.float32).reshape(CACHE_LENGTH, KEY_VALUE_HEADS, HEAD_SIZE)
    head_picker = jnp.arange(KEY_VALUE_HEADS, dtype=jnp.int32)[None, :, None, None]

    def attend(leading_row):
        query_matrix = lax.dynamic_slice_in_dim(queries, leading_row, rows_per_block, 0)
        query_head_rows = query_matrix.astype(jnp.float32).reshape(count_of_queries, PATTERN_BLOCK, KEY_VALUE_HEADS, head_groups, HEAD_SIZE)
        self_keys = lax.dynamic_slice_in_dim(fresh_keys, leading_row, rows_per_block, 0).astype(jnp.float32).reshape(count_of_queries, PATTERN_BLOCK, KEY_VALUE_HEADS, HEAD_SIZE)
        self_values = lax.dynamic_slice_in_dim(fresh_values, leading_row, rows_per_block, 0).astype(jnp.float32).reshape(count_of_queries, PATTERN_BLOCK, KEY_VALUE_HEADS, HEAD_SIZE)
        stream = lax.dynamic_slice_in_dim(residual, leading_row, rows_per_block, 0).astype(jnp.float32)
        query_block = ((CACHE_LENGTH + leading_row) // PATTERN_BLOCK + jnp.arange(count_of_queries, dtype=jnp.int32)).astype(jnp.int32)
        listed, usable = candidates(query_block, column_blocks, diagonal_offsets, block_total)
        row_index = (jnp.clip(listed, 0, block_total - 1)[..., None] * PATTERN_BLOCK + jnp.arange(PATTERN_BLOCK, dtype=jnp.int32)).astype(jnp.int32)
        key_rows = key_head_rows[row_index, head_picker]
        value_rows = value_head_rows[row_index, head_picker]
        scores = jnp.einsum('qthgd,qhcjd->qthgcj', query_head_rows, key_rows) * score_scale
        own_score = jnp.einsum('qthgd,qthd->qthg', query_head_rows, self_keys) * score_scale
        kept = usable[:, None, :, None, :, None]
        masked = jnp.where(kept, scores, -jnp.inf)
        top = jnp.maximum(own_score, lax.optimization_barrier(jnp.max(masked, axis=(-2, -1))))
        weights = jnp.where(kept, jnp.exp(scores - top[..., None, None]), 0.0).astype(jnp.bfloat16)
        weights = lax.optimization_barrier(weights).astype(jnp.float32)
        own_weight = jnp.exp(own_score - top).astype(jnp.bfloat16)
        own_weight = lax.optimization_barrier(own_weight).astype(jnp.float32)
        numer = own_weight[..., None] * self_values[:, :, :, None, :] + jnp.einsum('qthgcj,qhcjd->qthgd', weights, value_rows)
        denom = own_weight + lax.optimization_barrier(jnp.sum(weights, axis=(-2, -1)))
        attended = (numer / denom[..., None]).reshape(rows_per_block, QUERY_HEADS * HEAD_SIZE)
        hidden = stream + attended
        spread = lax.optimization_barrier(jnp.mean(hidden * hidden, axis=-1, keepdims=True))
        normed = (hidden * lax.rsqrt(spread + 1e-06) * norm_gain).astype(jnp.bfloat16)
        return (hidden, normed)
    starts = (jnp.arange(TOKEN_COUNT // rows_per_block, dtype=jnp.int32) * rows_per_block).astype(jnp.int32)
    hidden, normed = lax.map(attend, starts)
    hidden = hidden.reshape(TOKEN_COUNT, QUERY_HEADS * HEAD_SIZE)
    normed = normed.reshape(TOKEN_COUNT, QUERY_HEADS * HEAD_SIZE)
    flat_ids = routes.reshape(-1).astype(jnp.int32)
    flat_tokens = (jnp.arange(TOKEN_COUNT * TOP, dtype=jnp.int32) // TOP).astype(jnp.int32)
    flat_gates = gate_weights.reshape(-1)
    most_load = N_CTX * N_EXP * CAP

    def per_expert(expert_mix, expert):
        matches = flat_ids == expert
        picks_order = jnp.argsort(jnp.where(matches, 0, 1).astype(jnp.int32), stable=True)[:most_load].astype(jnp.int32)
        is_live = matches[picks_order]
        token_ids = flat_tokens[picks_order]
        rows = normed[token_ids]
        gate_part = jnp.dot(rows, w_gate[expert], preferred_element_type=jnp.float32)
        up_part = jnp.dot(rows, w_up[expert], preferred_element_type=jnp.float32)
        act = (jax.nn.silu(gate_part) * up_part).astype(jnp.bfloat16)
        answer = jnp.dot(act, w_down[expert], preferred_element_type=jnp.float32).astype(jnp.bfloat16)
        weight = jnp.where(is_live, flat_gates[picks_order], 0.0)
        expert_mix = expert_mix.at[token_ids].add(weight[:, None] * answer.astype(jnp.float32))
        return (expert_mix, None)
    expert_mix, _ = lax.scan(per_expert, jnp.zeros((TOKEN_COUNT, QUERY_HEADS * HEAD_SIZE), jnp.float32), jnp.arange(N_CTX * N_EXP, dtype=jnp.int32))
    return (hidden + expert_mix).astype(jnp.bfloat16)
```

```python
import functools

import jax
import jax.numpy as jnp
from jax import lax
from jax.experimental import pallas as pl
from jax.experimental.pallas import tpu as pltpu
from jax.sharding import PartitionSpec as P

MESH = pl.DeviceIdType.MESH
BF16 = jnp.bfloat16
F32 = jnp.float32
BLOCK = 64
HEAD = 128
HEADS_KV = 2
GROUP = 16
VERT = 2
SLASH = 8
SLOTS = VERT + 2 * SLASH
TOK = 128
D = 4096
FF = 768
HALF = D // 2
CAP = 10
PLANE = 32
MSG = 8 * CAP
ROWS = 16 * MSG
ALL = PLANE * MSG
PIECE = 256
PIECES = HALF // PIECE
NEG = -1e30


def coords():
    ctx = lax.axis_index("ctx")
    exp = lax.axis_index("exp")
    return ((exp // 4) % 2) * 2 + ctx // 2, exp % 4, exp // 8, ctx % 2


def device(x, y, z, c):
    return ((x % 2) * 2 + c, z * 8 + (x // 2) * 4 + y)


def plane_index(x, y, c):
    return ((x % 2) * 2 + c) * 8 + (x // 2) * 4 + y


def ordered_offsets():
    left = [(dx, dy, dc) for dx in range(4) for dy in range(4) for dc in range(2) if dx or dy or dc]
    use = {}
    out = []

    def links(o):
        found = []
        for axis in range(2):
            if o[axis] == 1:
                found.append((axis, 1))
            elif o[axis] == 3:
                found.append((axis, -1))
            elif o[axis] == 2:
                found += [(axis, 1), (axis, -1)]
        return found

    while left:
        best = min(left, key=lambda o: (sum(2 * use.get(k, 0) + 1 for k in links(o)), -len(links(o)), o))
        left.remove(best)
        out.append(best)
        for k in links(best):
            use[k] = use.get(k, 0) + 1
    return out


OFFSETS = ordered_offsets()
COLUMN = [(1, 0), (3, 1), (2, 0), (3, 0), (1, 1), (2, 1), (0, 1)]


def to_plane(o):
    x, y, z, c = coords()
    return (x + o[0]) % 4, (y + o[1]) % 4, z, (c + o[2]) % 2


def from_plane(o):
    x, y, z, c = coords()
    return (x + 4 - o[0]) % 4, (y + 4 - o[1]) % 4, z, (c + 2 - o[2]) % 2


def to_column(o):
    x, y, z, c = coords()
    return x, y, (z + o[0]) % 4, (c + o[1]) % 2


def from_column(o):
    x, y, z, c = coords()
    return x, y, (z + 4 - o[0]) % 4, (c + 2 - o[1]) % 2


def greet_all():
    bar = pltpu.get_barrier_semaphore()
    for o in OFFSETS:
        pl.semaphore_signal(bar, inc=1, device_id=device(*to_plane(o)), device_id_type=MESH)
    for o in COLUMN[:-1]:
        pl.semaphore_signal(bar, inc=1, device_id=device(*to_column(o)), device_id_type=MESH)
    pl.semaphore_wait(bar, len(OFFSETS) + len(COLUMN) - 1)


def collect_kernel(cols, offs, keys, values, con, near):
    ctx = lax.axis_index("ctx")
    exp = lax.axis_index("exp")
    xl = ctx // 2

    def put(h, slot, block_a, block_b):
        near_a = block_a - 32 * ctx
        near_b = block_b - 32 * ctx
        local = jnp.where((near_a >= 0) & (near_a < 32), near_a, near_b)
        inside = (local >= 0) & (local < 32)
        start = pl.multiple_of(jnp.clip(local, 0, 31) * BLOCK, BLOCK)
        factor = jnp.where(inside, 1.0, 0.0).astype(BF16)
        for kind, ref in ((0, keys), (1, values)):
            block = ref[pl.ds(start, BLOCK), h * HEAD : (h + 1) * HEAD]
            con[kind, h, slot * BLOCK : (slot + 1) * BLOCK, :] = block * factor

    for h in range(HEADS_KV):
        for v in range(VERT):
            put(h, v, cols[h, v], cols[h, v])
            here = (cols[h, v] // 64) == xl
            near[h * SLOTS + v] = jnp.full((8, HEAD), jnp.where(here, 1.0, 0.0), F32)
        for i in range(2):
            for s in range(SLASH):
                block_2 = 256 + 2 * exp + i - offs[h, s]
                slot = VERT + i * SLASH + s
                put(h, slot, block_2, block_2 + 64)
                near[h * SLOTS + slot] = jnp.full((8, HEAD), jnp.where(block_2 >= 0, 1.0, 0.0), F32)


def collect(cols, offs, keys, values):
    return pl.pallas_call(
        collect_kernel,
        name="collect_blocks",
        out_shape=[
            jax.ShapeDtypeStruct((2, HEADS_KV, SLOTS * BLOCK, HEAD), BF16),
            jax.ShapeDtypeStruct((HEADS_KV * SLOTS, 8, HEAD), F32),
        ],
        in_specs=[pl.BlockSpec(memory_space=pltpu.SMEM)] * 2 + [pl.BlockSpec(memory_space=pltpu.VMEM)] * 2,
        out_specs=[pl.BlockSpec(memory_space=pltpu.VMEM)] * 2,
        compiler_params=pltpu.CompilerParams(vmem_limit_bytes=16 * 2**20),
    )(cols, offs, keys, values)


def exchange_kernel(con, near, out, sib, chip, rem, fin, arr, ssem, rsem):
    x, y, z, c = coords()
    xl = x % 2
    exp = lax.axis_index("exp")
    twin = (xl * 2 + 1 - c, exp)
    across = ((1 - xl) * 2 + c, exp)
    bar = pltpu.get_barrier_semaphore()
    for other in (twin, across):
        pl.semaphore_signal(bar, inc=1, device_id=other, device_id_type=MESH)
    pl.semaphore_wait(bar, 2)

    first = pltpu.make_async_remote_copy(
        src_ref=con.at[1 - c], dst_ref=sib, send_sem=ssem.at[0], recv_sem=rsem.at[0],
        device_id=twin, device_id_type=MESH,
    )
    first.start()
    first.wait()
    chip[...] = con[c] + sib[...]

    verts = VERT * BLOCK

    def whole(h):
        return pltpu.make_async_remote_copy(
            src_ref=chip.at[h], dst_ref=rem.at[h], send_sem=ssem.at[1 + h], recv_sem=rsem.at[1 + h],
            device_id=across, device_id_type=MESH,
        )

    def vertical(h):
        return pltpu.make_async_remote_copy(
            src_ref=chip.at[h, pl.ds(0, verts)], dst_ref=rem.at[h, pl.ds(0, verts)],
            send_sem=ssem.at[1 + h], recv_sem=rsem.at[1 + h],
            device_id=across, device_id_type=MESH,
        )

    @pl.when(xl == 0)
    def _():
        for h in range(HEADS_KV):
            whole(h).start()

    @pl.when(xl == 1)
    def _():
        for h in range(HEADS_KV):
            vertical(h).start()

    def back(h):
        return pltpu.make_async_remote_copy(
            src_ref=fin.at[h], dst_ref=arr.at[h], send_sem=ssem.at[3 + h], recv_sem=rsem.at[3 + h],
            device_id=twin, device_id_type=MESH,
        )

    def pick(h, slot):
        span = slice(slot * BLOCK, (slot + 1) * BLOCK)
        local = near[h * SLOTS + slot, 0:1, :].astype(BF16)
        far = rem[h, span, :]
        return span, chip[h, span, :] * local + far * (1.0 - local).astype(BF16), far

    def pick_verticals(h):
        for v in range(VERT):
            span, mixed, _ = pick(h, v)
            fin[h, span, :] = mixed
            out[c, h, span, :] = mixed

    for h in range(HEADS_KV):

        @pl.when(xl == 0)
        def _():
            vertical(h).wait_recv()
            pick_verticals(h)
            fin[h, verts:, :] = jnp.zeros((2 * SLASH * BLOCK, HEAD), BF16)
            out[c, h, verts:, :] = jnp.zeros((2 * SLASH * BLOCK, HEAD), BF16)

        @pl.when(xl == 1)
        def _():
            whole(h).wait_recv()
            pick_verticals(h)
            for slot in range(VERT, SLOTS):
                span, mixed, far = pick(h, slot)

                @pl.when(c == 1)
                def _():
                    out[1, h, span, :] = mixed
                    fin[h, span, :] = far

                @pl.when(c == 0)
                def _():
                    out[0, h, span, :] = far
                    fin[h, span, :] = mixed

        back(h).start()

    for h in range(HEADS_KV):
        back(h).wait()
        out[1 - c, h] = arr[h]

    @pl.when(xl == 0)
    def _():
        for h in range(HEADS_KV):
            whole(h).wait_send()

    @pl.when(xl == 1)
    def _():
        for h in range(HEADS_KV):
            vertical(h).wait_send()


def exchange(con, near):
    part = (HEADS_KV, SLOTS * BLOCK, HEAD)
    return pl.pallas_call(
        exchange_kernel,
        name="key_exchange",
        out_shape=jax.ShapeDtypeStruct((2,) + part, BF16),
        in_specs=[pl.BlockSpec(memory_space=pltpu.VMEM)] * 2,
        out_specs=pl.BlockSpec(memory_space=pltpu.VMEM),
        scratch_shapes=[
            pltpu.VMEM(part, BF16),
            pltpu.VMEM(part, BF16),
            pltpu.VMEM(part, BF16),
            pltpu.VMEM(part, BF16),
            pltpu.VMEM(part, BF16),
            pltpu.SemaphoreType.DMA((5,)),
            pltpu.SemaphoreType.DMA((5,)),
        ],
        compiler_params=pltpu.CompilerParams(
            collective_id=1, has_side_effects=True, vmem_limit_bytes=24 * 2**20
        ),
    )(con, near)


def attend_kernel(cols, offs, q, fk, fv, kv, res, gain, routes, gates, hidden, normed, code, weight):
    ctx = lax.axis_index("ctx")
    exp = lax.axis_index("exp")
    scale = 1.0 / HEAD**0.5
    lane = lax.broadcasted_iota(jnp.int32, (1, (VERT + SLASH) * BLOCK), 1) // BLOCK
    heads = 4
    ones = jnp.ones(((VERT + SLASH) * BLOCK, HEAD), BF16)
    for h in range(HEADS_KV):
        for i in range(2):
            block = 128 + 2 * (ctx * 32 + exp) + i
            listed = [cols[h, v] for v in range(VERT)] + [block - offs[h, s] for s in range(SLASH)]
            bias = jnp.zeros(lane.shape, F32)
            for n, one in enumerate(listed):
                kept = (one >= 0) & (one < 128)
                for before in listed[:n]:
                    kept = kept & (one != before)
                bias = jnp.where(lane == n, jnp.where(kept, 0.0, NEG), bias)
            slash = VERT * BLOCK + i * SLASH * BLOCK
            k = jnp.concatenate([kv[0, h, : VERT * BLOCK, :], kv[0, h, slash : slash + SLASH * BLOCK, :]], axis=0)
            v = jnp.concatenate([kv[1, h, : VERT * BLOCK, :], kv[1, h, slash : slash + SLASH * BLOCK, :]], axis=0)
            v = jnp.concatenate([v, ones], axis=1)
            rows = slice(i * BLOCK, (i + 1) * BLOCK)
            own_k = fk[rows, h * HEAD : (h + 1) * HEAD].astype(F32)
            own_v = fv[rows, h * HEAD : (h + 1) * HEAD].astype(F32)
            own_k = jnp.concatenate([own_k] * heads, axis=0)
            own_v = jnp.concatenate([own_v] * heads, axis=0)
            for g in range(0, GROUP, heads):
                spans = [slice((h * GROUP + g + n) * HEAD, (h * GROUP + g + n + 1) * HEAD) for n in range(heads)]
                part = jnp.concatenate([q[rows, span] for span in spans], axis=0)
                scores = lax.dot_general(part, k, (((1,), (1,)), ((), ())), preferred_element_type=F32)
                scores = scores * scale + bias
                own = jnp.sum(part.astype(F32) * own_k, axis=1, keepdims=True) * scale
                top = jnp.maximum(own, jnp.max(scores, axis=1, keepdims=True))
                weights = jnp.exp(scores - top).astype(BF16)
                own_weight = jnp.exp(own - top).astype(BF16).astype(F32)
                both = jnp.dot(weights, v, preferred_element_type=F32)
                numer = both[:, :HEAD] + own_weight * own_v
                denom = both[:, HEAD:] + own_weight
                attended = numer / denom
                for n, span in enumerate(spans):
                    hidden[rows, span] = res[rows, span].astype(F32) + attended[n * BLOCK : (n + 1) * BLOCK]

    for r in range(0, TOK, 16):
        part = hidden[r : r + 16, :]
        spread = jnp.mean(part * part, axis=1, keepdims=True)
        normed[r : r + 16, :] = (part * lax.rsqrt(spread + 1e-6) * gain[...]).astype(BF16)

    ids = routes[...]
    ids = ((ids // 8) % 4) * 32 + (ids // 32) * 8 + ids % 8
    lanes = lax.broadcasted_iota(jnp.int32, (TOK, TOK), 1)
    named = jnp.zeros((TOK, TOK), F32)
    strength = jnp.zeros((TOK, TOK), F32)
    for n in range(8):
        hit = ids[:, n : n + 1] == lanes
        named = named + jnp.where(hit, 1.0, 0.0)
        strength = strength + jnp.where(hit, gates[:, n : n + 1], 0.0)
    earlier = (lanes < lax.broadcasted_iota(jnp.int32, (TOK, TOK), 0)).astype(BF16)
    place = jnp.dot(earlier, named.astype(BF16), preferred_element_type=F32)
    code[...] = jnp.where(named > 0.5, place, -1.0).T.astype(BF16)
    weight[...] = strength.T.astype(BF16)


def attend(cols, offs, q, fk, fv, kv, res, gain, routes, gates):
    return pl.pallas_call(
        attend_kernel,
        name="attention",
        out_shape=[
            jax.ShapeDtypeStruct((TOK, D), F32),
            jax.ShapeDtypeStruct((TOK, D), BF16),
            jax.ShapeDtypeStruct((TOK, TOK), BF16),
            jax.ShapeDtypeStruct((TOK, TOK), BF16),
        ],
        in_specs=[pl.BlockSpec(memory_space=pltpu.SMEM)] * 2 + [pl.BlockSpec(memory_space=pltpu.VMEM)] * 8,
        out_specs=[pl.BlockSpec(memory_space=pltpu.VMEM)] * 4,
        compiler_params=pltpu.CompilerParams(vmem_limit_bytes=32 * 2**20),
    )(cols, offs, q, fk, fv, kv, res, gain.reshape(1, D), routes, gates)


def table_rows():
    row = lax.broadcasted_iota(jnp.int32, (MSG, TOK), 0)
    block = jnp.zeros((MSG, TOK), jnp.int32)
    for b in range(1, 8):
        block = block + jnp.where(row >= b * CAP, 1, 0)
    return block, (row - block * CAP).astype(F32)


def dispatch_kernel(
    normed, code, weight, w_gate, w_up, act, codes_out, weights_out,
    x_all, codes, weights, select, stage, got, wg, wu, acc,
    wsem, tab_s, tab_r, col_s, col_r, msg_s, msg_r,
):
    x, y, z, c = coords()
    loads = [
        pltpu.make_async_copy(w_gate, wg, wsem.at[0]),
        pltpu.make_async_copy(w_up, wu, wsem.at[1]),
    ]
    for load in loads:
        load.start()
    greet_all()
    me = z * 2 + c

    def tables(n, o, dev, slot):
        return [
            pltpu.make_async_remote_copy(
                src_ref=src.at[dev[2]], dst_ref=dst.at[slot], send_sem=tab_s.at[t, n], recv_sem=tab_r.at[t, n],
                device_id=device(*dev), device_id_type=MESH,
            )
            for t, (src, dst) in enumerate(((code, codes), (weight, weights)))
        ]

    def column_copy(n, j, dev, slot):
        start = pl.multiple_of(dev[3] * HALF + j * PIECE, PIECE)
        return pltpu.make_async_remote_copy(
            src_ref=normed.at[:, pl.ds(start, PIECE)],
            dst_ref=x_all.at[j, pl.ds(pl.multiple_of(slot * TOK, TOK), TOK)],
            send_sem=col_s.at[j, n], recv_sem=col_r.at[j, n],
            device_id=device(*dev), device_id_type=MESH,
        )

    for n, o in enumerate(COLUMN):
        for one in tables(n, o, to_column(o), me):
            one.start()

    def send_columns(j, carry):
        for n, o in enumerate(COLUMN):
            column_copy(n, j, to_column(o), me).start()
        return carry

    lax.fori_loop(0, PIECES, send_columns, 0)

    mine = pl.ds(pl.multiple_of(me * TOK, TOK), TOK)
    for j in range(PIECES):
        start = pl.multiple_of(c * HALF + j * PIECE, PIECE)
        x_all[j, mine, :] = normed[:, pl.ds(start, PIECE)]
    codes[me] = code[z]
    weights[me] = weight[z]
    acc[...] = jnp.zeros_like(acc)

    for n, o in enumerate(COLUMN):
        dev = from_column(o)
        for one in tables(n, o, dev, dev[2] * 2 + dev[3]):
            one.wait()

    block, place = table_rows()
    codes_out[...] = codes[...].astype(F32)
    weights_out[...] = weights[...].astype(F32)

    def fill(l, carry):
        for b in range(8):
            row = codes_out[b, pl.ds(l, 1), :]
            hit = (row == place) & (block == b)
            select[pl.ds(pl.multiple_of(l * MSG, 16), MSG), b * TOK : (b + 1) * TOK] = jnp.where(hit, 1.0, 0.0).astype(BF16)
        return carry

    lax.fori_loop(0, PLANE, fill, 0)

    def message(k, j, dev, src_dev):
        to = plane_index(dev[0], dev[1], dev[3])
        chip = src_dev[0] * 4 + src_dev[1]
        return pltpu.make_async_remote_copy(
            src_ref=stage.at[j % 2, pl.ds(pl.multiple_of(to * MSG, 16), MSG)],
            dst_ref=got.at[j, src_dev[3], pl.ds(pl.multiple_of(chip * MSG, 16), MSG)],
            send_sem=msg_s.at[j, k], recv_sem=msg_r.at[j, k],
            device_id=device(*dev), device_id_type=MESH,
        )

    here = (x, y, z, c)
    own_rows = pl.ds(pl.multiple_of(plane_index(x, y, c) * MSG, 16), MSG)
    own_place = pl.ds(pl.multiple_of((x * 4 + y) * MSG, 16), MSG)

    def send_piece(j):
        for n, o in enumerate(COLUMN):
            dev = from_column(o)
            column_copy(n, j, dev, dev[2] * 2 + dev[3]).wait_recv()

        @pl.when(j >= 2)
        def _():
            for k, o in enumerate(OFFSETS):
                message(k, j - 2, to_plane(o), here).wait_send()

        step = ALL // 8

        def tile(t, carry):
            rows = pl.ds(pl.multiple_of(t * step, 16), step)
            stage[j % 2, rows, :] = jnp.dot(select[rows, :], x_all[j], preferred_element_type=F32).astype(BF16)
            return carry

        lax.fori_loop(0, 8, tile, 0)
        for k, o in enumerate(OFFSETS):
            message(k, j, to_plane(o), here).start()
        got[j, c, own_place, :] = stage[j % 2, own_rows, :]

    def use_piece(j):
        for k, o in enumerate(OFFSETS):
            message(k, j, here, from_plane(o)).wait_recv()
        low = pl.ds(pl.multiple_of(j * PIECE, PIECE), PIECE)
        high = pl.ds(pl.multiple_of(HALF + j * PIECE, PIECE), PIECE)
        step = ROWS // 5

        def tile(t, carry):
            rows = pl.ds(pl.multiple_of(t * step, 16), step)
            left = got[j, 0, rows, :]
            right = got[j, 1, rows, :]
            for n, w in enumerate((wg, wu)):
                acc[n, rows, :] += jnp.dot(left, w[low, :], preferred_element_type=F32) + jnp.dot(
                    right, w[high, :], preferred_element_type=F32
                )
            return carry

        lax.fori_loop(0, 5, tile, 0)

    def step(j, carry):
        @pl.when(j < PIECES)
        def _():
            send_piece(j)

        @pl.when(j == 1)
        def _():
            for load in loads:
                load.wait()

        @pl.when(j >= 1)
        def _():
            use_piece(j - 1)

        return carry

    lax.fori_loop(0, PIECES + 1, step, 0)

    def finish(t, carry):
        rows = pl.ds(pl.multiple_of(t * MSG, 16), MSG)
        g = acc[0, rows, :]
        act[rows, :] = (g / (1.0 + jnp.exp(-g)) * acc[1, rows, :]).astype(BF16)
        return carry

    lax.fori_loop(0, ROWS // MSG, finish, 0)

    for j in (PIECES - 2, PIECES - 1):
        for k, o in enumerate(OFFSETS):
            message(k, j, to_plane(o), here).wait_send()

    def sent_columns(j, carry):
        for n, o in enumerate(COLUMN):
            column_copy(n, j, to_column(o), me).wait_send()
        return carry

    lax.fori_loop(0, PIECES, sent_columns, 0)


def dispatch(normed, code, weight, w_gate, w_up):
    vmem = pl.BlockSpec(memory_space=pltpu.VMEM)
    hbm = pl.BlockSpec(memory_space=pl.ANY)
    dma = pltpu.SemaphoreType.DMA
    return pl.pallas_call(
        dispatch_kernel,
        name="dispatch",
        out_shape=[
            jax.ShapeDtypeStruct((ROWS, FF), BF16),
            jax.ShapeDtypeStruct((8, PLANE, TOK), F32),
            jax.ShapeDtypeStruct((8, PLANE, TOK), F32),
        ],
        in_specs=[vmem, vmem, vmem, hbm, hbm],
        out_specs=[vmem] * 3,
        scratch_shapes=[
            pltpu.VMEM((PIECES, 8 * TOK, PIECE), BF16),
            pltpu.VMEM((8, PLANE, TOK), BF16),
            pltpu.VMEM((8, PLANE, TOK), BF16),
            pltpu.VMEM((ALL, 8 * TOK), BF16),
            pltpu.VMEM((2, ALL, PIECE), BF16),
            pltpu.VMEM((PIECES, 2, ROWS, PIECE), BF16),
            pltpu.VMEM((D, FF), BF16),
            pltpu.VMEM((D, FF), BF16),
            pltpu.VMEM((2, ROWS, FF), F32),
            dma((2,)),
            dma((2, len(COLUMN))),
            dma((2, len(COLUMN))),
            dma((PIECES, len(COLUMN))),
            dma((PIECES, len(COLUMN))),
            dma((PIECES, len(OFFSETS))),
            dma((PIECES, len(OFFSETS))),
        ],
        compiler_params=pltpu.CompilerParams(
            collective_id=2, has_side_effects=True, vmem_limit_bytes=60 * 2**20
        ),
    )(normed, code.reshape(4, PLANE, TOK), weight.reshape(4, PLANE, TOK), w_gate, w_up)


def combine_kernel(
    act, codes, weights, w_down, hidden, out,
    wd, answers, got, mix, partial, sums,
    wsem, msg_s, msg_r, col_s, col_r,
):
    x, y, z, c = coords()
    load = pltpu.make_async_copy(w_down, wd, wsem.at[0])
    load.start()
    greet_all()
    load.wait()
    here = (x, y, z, c)
    me = z * 2 + c

    def message(k, j, dev, src_dev):
        chip = dev[0] * 4 + dev[1]
        of = plane_index(src_dev[0], src_dev[1], src_dev[3])
        return pltpu.make_async_remote_copy(
            src_ref=answers.at[j, dev[3], pl.ds(pl.multiple_of(chip * MSG, 16), MSG)],
            dst_ref=got.at[j, pl.ds(pl.multiple_of(of * MSG, 16), MSG)],
            send_sem=msg_s.at[j, k], recv_sem=msg_r.at[j, k],
            device_id=device(*dev), device_id_type=MESH,
        )

    def column_copy(n, j, dev, src_dev):
        block = dev[2] * 2 + dev[3]
        return pltpu.make_async_remote_copy(
            src_ref=partial.at[j, pl.ds(pl.multiple_of(block * TOK, TOK), TOK)],
            dst_ref=sums.at[j, src_dev[2], src_dev[3]],
            send_sem=col_s.at[j, n], recv_sem=col_r.at[j, n],
            device_id=device(*dev), device_id_type=MESH,
        )

    own_rows = pl.ds(pl.multiple_of(plane_index(x, y, c) * MSG, 16), MSG)
    own_place = pl.ds(pl.multiple_of((x * 4 + y) * MSG, 16), MSG)

    def send_piece(j, carry):
        for half in range(2):
            span = pl.ds(pl.multiple_of(half * HALF + j * PIECE, PIECE), PIECE)

            def tile(t, inner):
                rows = pl.ds(pl.multiple_of(t * (ROWS // 4), 16), ROWS // 4)
                answers[j, half, rows, :] = jnp.dot(act[rows, :], wd[:, span], preferred_element_type=F32).astype(BF16)
                return inner

            lax.fori_loop(0, 4, tile, 0)
        for k, o in enumerate(OFFSETS):
            message(k, j, to_plane(o), here).start()
        got[j, own_rows, :] = answers[j, c, own_place, :]
        return carry

    lax.fori_loop(0, PIECES, send_piece, 0)

    block, place = table_rows()

    def fill(p, carry):
        for b in range(8):
            rows = []
            for n in range(8):
                l = p * 8 + n
                hit = (codes[b, pl.ds(l, 1), :] == place) & (block == b)
                rows.append(jnp.where(hit, weights[b, pl.ds(l, 1), :], 0.0))
            whole = jnp.concatenate(rows, axis=0)
            mix[b * TOK : (b + 1) * TOK, pl.ds(pl.multiple_of(p * 8 * MSG, TOK), 8 * MSG)] = whole.T.astype(BF16)
        return carry

    lax.fori_loop(0, PLANE // 8, fill, 0)

    def reduce_piece(j):
        for k, o in enumerate(OFFSETS):
            message(k, j, here, from_plane(o)).wait_recv()

        def tile(t, carry):
            rows = pl.ds(pl.multiple_of(t * 256, 256), 256)
            partial[j, rows, :] = jnp.dot(mix[rows, :], got[j], preferred_element_type=F32).astype(BF16)
            return carry

        lax.fori_loop(0, 4, tile, 0)
        for n, o in enumerate(COLUMN):
            column_copy(n, j, to_column(o), here).start()
        sums[j, z, c] = partial[j, pl.ds(pl.multiple_of(me * TOK, TOK), TOK), :]

    def finish_piece(j):
        for n, o in enumerate(COLUMN):
            column_copy(n, j, here, from_column(o)).wait_recv()
        for half in range(2):
            span = pl.ds(pl.multiple_of(half * HALF + j * PIECE, PIECE), PIECE)
            total = hidden[:, span]
            for n in range(4):
                total = total + sums[j, n, half].astype(F32)
            out[:, span] = total.astype(BF16)

    def step(j, carry):
        @pl.when(j < PIECES)
        def _():
            reduce_piece(j)

        @pl.when(j >= 1)
        def _():
            finish_piece(j - 1)

        return carry

    lax.fori_loop(0, PIECES + 1, step, 0)

    def sent(j, carry):
        for k, o in enumerate(OFFSETS):
            message(k, j, to_plane(o), here).wait_send()
        for n, o in enumerate(COLUMN):
            column_copy(n, j, to_column(o), here).wait_send()
        return carry

    lax.fori_loop(0, PIECES, sent, 0)


def combine(act, codes, weights, w_down, hidden):
    vmem = pl.BlockSpec(memory_space=pltpu.VMEM)
    dma = pltpu.SemaphoreType.DMA
    return pl.pallas_call(
        combine_kernel,
        name="combine",
        out_shape=jax.ShapeDtypeStruct((TOK, D), BF16),
        in_specs=[vmem, vmem, vmem, pl.BlockSpec(memory_space=pl.ANY), vmem],
        out_specs=vmem,
        scratch_shapes=[
            pltpu.VMEM((FF, D), BF16),
            pltpu.VMEM((PIECES, 2, ROWS, PIECE), BF16),
            pltpu.VMEM((PIECES, ALL, PIECE), BF16),
            pltpu.VMEM((8 * TOK, ALL), BF16),
            pltpu.VMEM((PIECES, 8 * TOK, PIECE), BF16),
            pltpu.VMEM((PIECES, 4, 2, TOK, PIECE), BF16),
            dma((1,)),
            dma((PIECES, len(OFFSETS))),
            dma((PIECES, len(OFFSETS))),
            dma((PIECES, len(COLUMN))),
            dma((PIECES, len(COLUMN))),
        ],
        compiler_params=pltpu.CompilerParams(
            collective_id=3, has_side_effects=True, vmem_limit_bytes=60 * 2**20
        ),
    )(act, codes, weights, w_down, hidden)


def body(
    queries, fresh_keys, fresh_values, stored_keys, stored_values, column_blocks, diagonal_offsets,
    residual, norm_gain, routes, gate_weights, w_gate, w_up, w_down,
):
    kv = exchange(*collect(column_blocks, diagonal_offsets, stored_keys, stored_values))
    hidden, normed, code, weight = attend(
        column_blocks, diagonal_offsets, queries, fresh_keys, fresh_values, kv,
        residual, norm_gain, routes, gate_weights,
    )
    act, codes, weights = dispatch(normed, code, weight, w_gate[0], w_up[0])
    return combine(act, codes, weights, w_down[0], hidden)


def solution(mesh):
    rows = P(("ctx", "exp"), None)
    experts = P(("ctx", "exp"), None, None)
    in_specs = (
        rows, rows, rows, P("ctx", None), P("ctx", None), P(), P(), rows, P(), rows, rows,
        experts, experts, experts,
    )
    return jax.shard_map(body, mesh=mesh, in_specs=in_specs, out_specs=rows, check_vma=False)
```

```python
import functools

import jax
import jax.numpy as jnp
from jax import lax
from jax.experimental import pallas as pl
from jax.experimental.pallas import tpu as pltpu
from jax.sharding import PartitionSpec as P

MESH = pl.DeviceIdType.MESH
BF16 = jnp.bfloat16
F32 = jnp.float32
BLOCK = 64
HEAD = 128
HEADS_KV = 2
GROUP = 16
VERT = 2
SLASH = 8
SLOTS = VERT + 2 * SLASH
TOK = 128
D = 4096
FF = 768
HALF = D // 2
CAP = 10
PLANE = 32
MSG = 8 * CAP
ROWS = 16 * MSG
ALL = PLANE * MSG
PIECE = 256
PIECES = HALF // PIECE
NEG = -1e30


TYPES = 3


def coords():
    ctx = lax.axis_index("ctx")
    exp = lax.axis_index("exp")
    return ((exp // 4) % 2) * 2 + ctx // 2, exp % 4, exp // 8, ctx % 2


def device(x, y, z, c):
    return ((x % 2) * 2 + c, z * 8 + (x // 2) * 4 + y)


def unit(t):
    return (2 - t) * (1 - t) // 2, t * (2 - t), t * (t - 1) // 2


def turned(t):
    x, y, z, c = coords()
    t0, t1, t2 = unit(t)
    return x * (t0 + t1) + y * t2, y * t0 + z * (t1 + t2), z * t0 + y * t1 + x * t2, c


def turned_device(t, dev):
    p, q, a, c = dev
    t0, t1, t2 = unit(t)
    return device(p * (t0 + t1) + a * t2, q * t0 + a * t1 + p * t2, a * t0 + q * (t1 + t2), c)


def plane_index(dev):
    return (dev[0] * 4 + dev[1]) * 2 + dev[3]


def ordered_offsets():
    left = [(dx, dy, dc) for dx in range(4) for dy in range(4) for dc in range(2) if dx or dy or dc]
    use = {}
    out = []

    def links(o):
        found = []
        for axis in range(2):
            if o[axis] == 1:
                found.append((axis, 1))
            elif o[axis] == 3:
                found.append((axis, -1))
            elif o[axis] == 2:
                found += [(axis, 1), (axis, -1)]
        return found

    while left:
        best = min(left, key=lambda o: (sum(2 * use.get(k, 0) + 1 for k in links(o)), -len(links(o)), o))
        left.remove(best)
        out.append(best)
        for k in links(best):
            use[k] = use.get(k, 0) + 1
    return out


OFFSETS = ordered_offsets()
COLUMN = [(1, 0), (3, 1), (2, 0), (3, 0), (1, 1), (2, 1), (0, 1)]
PEERS = [
    (dx, dy, dz, dc)
    for dx in range(4)
    for dy in range(4)
    for dz in range(4)
    for dc in range(2)
    if dx * dy * dz == 0 and (dx or dy or dz or dc)
]


def to_plane(o, dev):
    return (dev[0] + o[0]) % 4, (dev[1] + o[1]) % 4, dev[2], (dev[3] + o[2]) % 2


def from_plane(o, dev):
    return (dev[0] + 4 - o[0]) % 4, (dev[1] + 4 - o[1]) % 4, dev[2], (dev[3] + 2 - o[2]) % 2


def to_column(o, dev):
    return dev[0], dev[1], (dev[2] + o[0]) % 4, (dev[3] + o[1]) % 2


def from_column(o, dev):
    return dev[0], dev[1], (dev[2] + 4 - o[0]) % 4, (dev[3] + 2 - o[1]) % 2


def greet_all():
    bar = pltpu.get_barrier_semaphore()
    x, y, z, c = coords()
    for o in PEERS:
        other = device((x + o[0]) % 4, (y + o[1]) % 4, (z + o[2]) % 4, (c + o[3]) % 2)
        pl.semaphore_signal(bar, inc=1, device_id=other, device_id_type=MESH)
    pl.semaphore_wait(bar, len(PEERS))


def digits(row):
    n = (row * 3277) >> 16
    return n >> 4, (n >> 2) & 3, n & 3, row - n * 20


def swap_matrix():
    row = lax.broadcasted_iota(jnp.int32, (320, 1), 0)
    _, d2, d1, rest = digits(row)
    source = d1 * 80 + d2 * 20 + rest
    return (lax.broadcasted_iota(jnp.int32, (320, 320), 1) == source).astype(F32).astype(BF16)


def turn_matrix(rows, start, back):
    row = lax.broadcasted_iota(jnp.int32, (rows, 1), 0) + start
    d3, d2, d1, rest = digits(row)
    source = d1 * 320 + d3 * 80 + d2 * 20 + rest if back else d2 * 320 + d1 * 80 + d3 * 20 + rest
    return (lax.broadcasted_iota(jnp.int32, (rows, ROWS), 1) == source).astype(F32).astype(BF16)


def side(h):
    exp = lax.axis_index("exp")
    return exp + h * (4 - 8 * ((exp // 4) % 2))


def collect_kernel(cols, offs, keys_hbm, values_hbm, con, near, keys, values, sem):
    loads = [pltpu.make_async_copy(keys_hbm, keys, sem.at[0]), pltpu.make_async_copy(values_hbm, values, sem.at[1])]
    for load in loads:
        load.start()
    ctx = lax.axis_index("ctx")
    xl = ctx // 2
    for load in loads:
        load.wait()

    def put(h, slot, block_a, block_b):
        near_a = block_a - 32 * ctx
        near_b = block_b - 32 * ctx
        local = jnp.where((near_a >= 0) & (near_a < 32), near_a, near_b)
        inside = (local >= 0) & (local < 32)
        start = pl.multiple_of(jnp.clip(local, 0, 31) * BLOCK, BLOCK)
        factor = jnp.where(inside, 1.0, 0.0).astype(BF16)
        for kind, ref in ((0, keys), (1, values)):
            block = ref[pl.ds(start, BLOCK), h * HEAD : (h + 1) * HEAD]
            con[kind, h, slot * BLOCK : (slot + 1) * BLOCK, :] = block * factor

    for h in range(HEADS_KV):
        exp = jnp.where(xl == 0, side(h), side(0))
        for v in range(VERT):
            put(h, v, cols[h, v], cols[h, v])
            here = (cols[h, v] // 64) == xl
            near[h * SLOTS + v] = jnp.full((8, HEAD), jnp.where(here, 1.0, 0.0), F32)
        for i in range(2):
            for s in range(SLASH):
                block_2 = 256 + 2 * exp + i - offs[h, s]
                slot = VERT + i * SLASH + s
                put(h, slot, block_2, block_2 + 64)
                near[h * SLOTS + slot] = jnp.full((8, HEAD), jnp.where(block_2 >= 0, 1.0, 0.0), F32)


def collect(cols, offs, keys, values):
    return pl.pallas_call(
        collect_kernel,
        name="collect_blocks",
        out_shape=[
            jax.ShapeDtypeStruct((2, HEADS_KV, SLOTS * BLOCK, HEAD), BF16),
            jax.ShapeDtypeStruct((HEADS_KV * SLOTS, 8, HEAD), F32),
        ],
        in_specs=[pl.BlockSpec(memory_space=pltpu.SMEM)] * 2 + [pl.BlockSpec(memory_space=pltpu.HBM)] * 2,
        out_specs=[pl.BlockSpec(memory_space=pltpu.VMEM)] * 2,
        scratch_shapes=[
            pltpu.VMEM((2048, HEADS_KV * HEAD), BF16),
            pltpu.VMEM((2048, HEADS_KV * HEAD), BF16),
            pltpu.SemaphoreType.DMA((2,)),
        ],
        compiler_params=pltpu.CompilerParams(vmem_limit_bytes=16 * 2**20),
    )(cols, offs, keys, values)


def exchange_kernel(con, near, out, sib, chip, rem, fin, arr, ssem, rsem):
    x, y, z, c = coords()
    xl = x % 2
    exp = lax.axis_index("exp")
    twin = (xl * 2 + 1 - c, exp)
    across = [((1 - xl) * 2 + c, side(h)) for h in range(HEADS_KV)]
    bar = pltpu.get_barrier_semaphore()
    for other in (twin, *across):
        pl.semaphore_signal(bar, inc=1, device_id=other, device_id_type=MESH)
    pl.semaphore_wait(bar, 3)

    first = pltpu.make_async_remote_copy(
        src_ref=con.at[1 - c], dst_ref=sib, send_sem=ssem.at[0], recv_sem=rsem.at[0],
        device_id=twin, device_id_type=MESH,
    )
    first.start()
    first.wait()
    chip[...] = con[c] + sib[...]

    verts = VERT * BLOCK

    def whole(h):
        return pltpu.make_async_remote_copy(
            src_ref=chip.at[h], dst_ref=rem.at[h], send_sem=ssem.at[1 + h], recv_sem=rsem.at[1 + h],
            device_id=across[h], device_id_type=MESH,
        )

    def vertical(h):
        return pltpu.make_async_remote_copy(
            src_ref=chip.at[h, pl.ds(0, verts)], dst_ref=rem.at[h, pl.ds(0, verts)],
            send_sem=ssem.at[1 + h], recv_sem=rsem.at[1 + h],
            device_id=across[h], device_id_type=MESH,
        )

    @pl.when(xl == 0)
    def _():
        for h in range(HEADS_KV):
            whole(h).start()

    @pl.when(xl == 1)
    def _():
        for h in range(HEADS_KV):
            vertical(h).start()

    def back(h):
        return pltpu.make_async_remote_copy(
            src_ref=fin.at[h], dst_ref=arr.at[h], send_sem=ssem.at[3 + h], recv_sem=rsem.at[3 + h],
            device_id=twin, device_id_type=MESH,
        )

    def pick(h, slot):
        span = slice(slot * BLOCK, (slot + 1) * BLOCK)
        local = near[h * SLOTS + slot, 0:1, :].astype(BF16)
        far = rem[h, span, :]
        return span, chip[h, span, :] * local + far * (1.0 - local).astype(BF16), far

    def pick_verticals(h):
        for v in range(VERT):
            span, mixed, _ = pick(h, v)
            fin[h, span, :] = mixed
            out[c, h, span, :] = mixed

    for h in range(HEADS_KV):

        @pl.when(xl == 0)
        def _():
            vertical(h).wait_recv()
            pick_verticals(h)
            fin[h, verts:, :] = jnp.zeros((2 * SLASH * BLOCK, HEAD), BF16)
            out[c, h, verts:, :] = jnp.zeros((2 * SLASH * BLOCK, HEAD), BF16)

        @pl.when(xl == 1)
        def _():
            whole(h).wait_recv()
            pick_verticals(h)
            for slot in range(VERT, SLOTS):
                span, mixed, far = pick(h, slot)

                @pl.when(c == 1)
                def _():
                    out[1, h, span, :] = mixed
                    fin[h, span, :] = far

                @pl.when(c == 0)
                def _():
                    out[0, h, span, :] = far
                    fin[h, span, :] = mixed

        back(h).start()

    for h in range(HEADS_KV):
        back(h).wait()
        out[1 - c, h] = arr[h]

    @pl.when(xl == 0)
    def _():
        for h in range(HEADS_KV):
            whole(h).wait_send()

    @pl.when(xl == 1)
    def _():
        for h in range(HEADS_KV):
            vertical(h).wait_send()


def exchange(con, near):
    part = (HEADS_KV, SLOTS * BLOCK, HEAD)
    return pl.pallas_call(
        exchange_kernel,
        name="key_exchange",
        out_shape=jax.ShapeDtypeStruct((2,) + part, BF16),
        in_specs=[pl.BlockSpec(memory_space=pltpu.VMEM)] * 2,
        out_specs=pl.BlockSpec(memory_space=pltpu.VMEM),
        scratch_shapes=[
            pltpu.VMEM(part, BF16),
            pltpu.VMEM(part, BF16),
            pltpu.VMEM(part, BF16),
            pltpu.VMEM(part, BF16),
            pltpu.VMEM(part, BF16),
            pltpu.SemaphoreType.DMA((5,)),
            pltpu.SemaphoreType.DMA((5,)),
        ],
        compiler_params=pltpu.CompilerParams(
            collective_id=1, has_side_effects=True, vmem_limit_bytes=24 * 2**20
        ),
    )(con, near)


def attend_kernel(
    cols, offs, q, fk, fv, kv, res, gain, routes, gates, hidden_out, normed_out, table_out,
    hidden, normed, table, sem,
):
    puts = []

    def put(src, dst):
        copy = pltpu.make_async_copy(src, dst, sem.at[len(puts)])
        copy.start()
        puts.append(copy)

    ctx = lax.axis_index("ctx")
    exp = lax.axis_index("exp")

    ids = routes[...]
    group, rest = ids >> 5, ids & 31
    ex, ey, ez, ec = ((rest >> 2) & 1) * 2 + (group >> 1), rest & 3, rest >> 3, group & 1
    lanes = lax.broadcasted_iota(jnp.int32, (TOK, TOK), 1)
    subs = lax.broadcasted_iota(jnp.int32, (TOK, TOK), 0)
    later = (subs < lanes).astype(F32).astype(BF16)
    for t, (p, r, a) in enumerate(((ex, ey, ez), (ex, ez, ey), (ey, ez, ex))):
        number = a * PLANE + (p * 4 + r) * 2 + ec
        named = jnp.zeros((TOK, TOK), F32)
        strength = jnp.zeros((TOK, TOK), F32)
        for n in range(8):
            hit = number[n : n + 1, :] == subs
            named = named + jnp.where(hit, 1.0, 0.0)
            strength = strength + jnp.where(hit, gates[n : n + 1, :], 0.0)
        place = jnp.dot(named.astype(BF16), later, preferred_element_type=F32)
        place = jnp.where(named > 0.5, place, -1.0).astype(BF16)
        strength = strength.astype(BF16)
        for n in range(4):
            table[t, n, 0] = place[n * PLANE : (n + 1) * PLANE]
            table[t, n, 1] = strength[n * PLANE : (n + 1) * PLANE]
    put(table, table_out)

    scale = 1.0 / HEAD**0.5
    lane = lax.broadcasted_iota(jnp.int32, (1, (VERT + SLASH) * BLOCK), 1) // BLOCK
    heads = 4
    ones = jnp.ones(((VERT + SLASH) * BLOCK, HEAD), BF16)
    for h in range(HEADS_KV):
        for i in range(2):
            block = 128 + 2 * (ctx * 32 + exp) + i
            listed = [cols[h, v] for v in range(VERT)] + [block - offs[h, s] for s in range(SLASH)]
            bias = jnp.zeros(lane.shape, F32)
            for n, one in enumerate(listed):
                kept = (one >= 0) & (one < 128)
                for before in listed[:n]:
                    kept = kept & (one != before)
                bias = jnp.where(lane == n, jnp.where(kept, 0.0, NEG), bias)
            slash = VERT * BLOCK + i * SLASH * BLOCK
            k = jnp.concatenate([kv[0, h, : VERT * BLOCK, :], kv[0, h, slash : slash + SLASH * BLOCK, :]], axis=0)
            v = jnp.concatenate([kv[1, h, : VERT * BLOCK, :], kv[1, h, slash : slash + SLASH * BLOCK, :]], axis=0)
            v = jnp.concatenate([v, ones], axis=1)
            rows = slice(i * BLOCK, (i + 1) * BLOCK)
            own_k = fk[rows, h * HEAD : (h + 1) * HEAD].astype(F32)
            own_v = fv[rows, h * HEAD : (h + 1) * HEAD].astype(F32)
            own_k = jnp.concatenate([own_k] * heads, axis=0)
            own_v = jnp.concatenate([own_v] * heads, axis=0)
            for g in range(0, GROUP, heads):
                spans = [slice((h * GROUP + g + n) * HEAD, (h * GROUP + g + n + 1) * HEAD) for n in range(heads)]
                part = jnp.concatenate([q[rows, span] for span in spans], axis=0)
                scores = lax.dot_general(part, k, (((1,), (1,)), ((), ())), preferred_element_type=F32)
                scores = scores * scale + bias
                own = jnp.sum(part.astype(F32) * own_k, axis=1, keepdims=True) * scale
                top = jnp.maximum(own, jnp.max(scores, axis=1, keepdims=True))
                weights = jnp.exp(scores - top).astype(BF16)
                own_weight = jnp.exp(own - top).astype(BF16).astype(F32)
                both = jnp.dot(weights, v, preferred_element_type=F32)
                numer = both[:, :HEAD] + own_weight * own_v
                denom = both[:, HEAD:] + own_weight
                attended = numer / denom
                for n, span in enumerate(spans):
                    hidden[rows, span] = res[rows, span].astype(F32) + attended[n * BLOCK : (n + 1) * BLOCK]
            done = hidden.at[pl.ds(i * BLOCK, BLOCK), pl.ds(h * GROUP * HEAD, GROUP * HEAD)]
            put(done, hidden_out.at[pl.ds(i * BLOCK, BLOCK), pl.ds(h * GROUP * HEAD, GROUP * HEAD)])

    for r in range(0, TOK, 16):
        part = hidden[r : r + 16, :]
        spread = jnp.mean(part * part, axis=1, keepdims=True)
        normed[r : r + 16, :] = (part * lax.rsqrt(spread + 1e-6) * gain[...]).astype(BF16)

    put(normed, normed_out)
    for copy in puts:
        copy.wait()


def attend(cols, offs, q, fk, fv, kv, res, gain, routes, gates):
    vmem = pl.BlockSpec(memory_space=pltpu.VMEM)
    shapes = [((TOK, D), F32), ((TOK, D), BF16), ((TYPES, 4, 2, PLANE, TOK), BF16)]
    return pl.pallas_call(
        attend_kernel,
        name="attention",
        out_shape=[jax.ShapeDtypeStruct(*one) for one in shapes],
        in_specs=[pl.BlockSpec(memory_space=pltpu.SMEM)] * 2 + [vmem] * 8,
        out_specs=[pl.BlockSpec(memory_space=pltpu.HBM)] * 3,
        scratch_shapes=[pltpu.VMEM(*one) for one in shapes] + [pltpu.SemaphoreType.DMA((6,))],
        compiler_params=pltpu.CompilerParams(vmem_limit_bytes=32 * 2**20),
    )(cols, offs, q, fk, fv, kv, res, gain.reshape(1, D), routes.T, gates.T)


def table_rows():
    row = lax.broadcasted_iota(jnp.int32, (MSG, TOK), 0)
    block = jnp.zeros((MSG, TOK), jnp.int32)
    for b in range(1, 8):
        block = block + jnp.where(row >= b * CAP, 1, 0)
    return block, (row - block * CAP).astype(F32)


def dispatch_kernel(
    normed_hbm, table_hbm, w_gate, w_up, act, tables_out,
    normed, table, x_all, tables, select, stage, got, weights, acc, swap, turn, sorted_rows,
    in_sem, w_sem, tab_s, tab_r, col_s, col_r, msg_s, msg_r,
):
    loads = [
        pltpu.make_async_copy(table_hbm, table, in_sem.at[0]),
        pltpu.make_async_copy(normed_hbm, normed, in_sem.at[1]),
    ]
    for load in loads:
        load.start()

    def weight_loads(j):
        return [
            pltpu.make_async_copy(
                w.at[pl.ds(pl.multiple_of(half * HALF + j * PIECE, PIECE), PIECE)],
                weights.at[j % 2, n, half],
                w_sem.at[j % 2, n, half],
            )
            for n, w in enumerate((w_gate, w_up))
            for half in range(2)
        ]

    for j in range(2):
        for load in weight_loads(j):
            load.start()
    greet_all()
    for load in loads:
        load.wait()

    def table_copy(n, t, dev, slot):
        return pltpu.make_async_remote_copy(
            src_ref=table.at[t, dev[2]], dst_ref=tables.at[t, slot], send_sem=tab_s.at[t, n], recv_sem=tab_r.at[t, n],
            device_id=turned_device(t, dev), device_id_type=MESH,
        )

    def column_copy(n, j, t, dev, slot):
        start = pl.multiple_of(dev[3] * HALF + j * PIECE, PIECE)
        return pltpu.make_async_remote_copy(
            src_ref=normed.at[:, pl.ds(start, PIECE)],
            dst_ref=x_all.at[j, pl.ds(pl.multiple_of(slot * TOK, TOK), TOK)],
            send_sem=col_s.at[j, n], recv_sem=col_r.at[j, n],
            device_id=turned_device(t, dev), device_id_type=MESH,
        )

    for t in range(TYPES):
        here = turned(t)
        me = here[2] * 2 + here[3]
        for n, o in enumerate(COLUMN):
            table_copy(n, t, to_column(o, here), me).start()
        tables[t, me] = table[t, here[2]]

    def send_columns(j, carry):
        t = j % 3
        here = turned(t)
        me = here[2] * 2 + here[3]
        for n, o in enumerate(COLUMN):
            column_copy(n, j, t, to_column(o, here), me).start()
        start = pl.multiple_of(here[3] * HALF + j * PIECE, PIECE)
        x_all[j, pl.ds(pl.multiple_of(me * TOK, TOK), TOK), :] = normed[:, pl.ds(start, PIECE)]
        return carry

    lax.fori_loop(0, PIECES, send_columns, 0)

    for t in range(TYPES):
        here = turned(t)
        for n, o in enumerate(COLUMN):
            dev = from_column(o, here)
            table_copy(n, t, dev, dev[2] * 2 + dev[3]).wait()
    tables_out[...] = tables[...].astype(F32)

    block, place = table_rows()

    def fill(t):
        def one(l, carry):
            for b in range(8):
                row = tables_out[t, b, 0, pl.ds(l, 1), :]
                hit = (row == place) & (block == b)
                select[t, pl.ds(pl.multiple_of(l * MSG, 16), MSG), b * TOK : (b + 1) * TOK] = jnp.where(
                    hit, 1.0, 0.0
                ).astype(BF16)
            return carry

        lax.fori_loop(0, PLANE, one, 0)

    fill(0)

    def message(k, j, t, dev, src_dev):
        chip = src_dev[0] * 4 + src_dev[1]
        return pltpu.make_async_remote_copy(
            src_ref=stage.at[j % 2, pl.ds(pl.multiple_of(plane_index(dev) * MSG, 16), MSG)],
            dst_ref=got.at[j, src_dev[3], pl.ds(pl.multiple_of(chip * MSG, 16), MSG)],
            send_sem=msg_s.at[j, k], recv_sem=msg_r.at[j, k],
            device_id=turned_device(t, dev), device_id_type=MESH,
        )

    def sent(j):
        here = turned(j % 3)
        for k, o in enumerate(OFFSETS):
            message(k, j, j % 3, to_plane(o, here), here).wait_send()

    def send_piece(j):
        t = j % 3
        here = turned(t)
        for n, o in enumerate(COLUMN):
            dev = from_column(o, here)
            column_copy(n, j, t, dev, dev[2] * 2 + dev[3]).wait_recv()

        @pl.when(j >= 2)
        def _():
            sent(j - 2)

        step = ALL // 8

        def tile(i, carry):
            rows = pl.ds(pl.multiple_of(i * step, 16), step)
            stage[j % 2, rows, :] = jnp.dot(select[t, rows, :], x_all[j], preferred_element_type=F32).astype(BF16)
            return carry

        lax.fori_loop(0, 8, tile, 0)
        for k, o in enumerate(OFFSETS):
            message(k, j, t, to_plane(o, here), here).start()
        own_rows = pl.ds(pl.multiple_of(plane_index(here) * MSG, 16), MSG)
        own_place = pl.ds(pl.multiple_of((here[0] * 4 + here[1]) * MSG, 16), MSG)
        got[j, here[3], own_place, :] = stage[j % 2, own_rows, :]

    def use_piece(j):
        t = j % 3
        here = turned(t)
        for load in weight_loads(j):
            load.wait()
        for k, o in enumerate(OFFSETS):
            message(k, j, t, here, from_plane(o, here)).wait_recv()

        @pl.when(t == 0)
        def _():
            sorted_rows[...] = got[j]

        @pl.when(t == 1)
        def _():
            for half in range(2):
                for i in range(4):
                    rows = slice(i * 320, (i + 1) * 320)
                    sorted_rows[half, rows, :] = jnp.dot(
                        swap[...], got[j, half, rows, :], preferred_element_type=F32
                    ).astype(BF16)

        @pl.when(t == 2)
        def _():
            def tile(i, carry):
                rows = pl.ds(pl.multiple_of(i * 320, 16), 320)
                for half in range(2):
                    sorted_rows[half, rows, :] = jnp.dot(
                        turn[rows, :], got[j, half], preferred_element_type=F32
                    ).astype(BF16)
                return carry

            lax.fori_loop(0, 4, tile, 0)

        step = ROWS // 5

        def tile(i, carry):
            rows = pl.ds(pl.multiple_of(i * step, 16), step)
            left = sorted_rows[0, rows, :]
            right = sorted_rows[1, rows, :]
            for n in range(2):
                acc[n, rows, :] += jnp.dot(left, weights[j % 2, n, 0], preferred_element_type=F32) + jnp.dot(
                    right, weights[j % 2, n, 1], preferred_element_type=F32
                )
            return carry

        lax.fori_loop(0, 5, tile, 0)

        @pl.when(j + 2 < PIECES)
        def _():
            for load in weight_loads(j + 2):
                load.start()

    def step(j, carry):
        @pl.when(j < PIECES)
        def _():
            send_piece(j)

        @pl.when(j == 0)
        def _():
            acc[...] = jnp.zeros_like(acc)
            swap[...] = swap_matrix()

            def tile(i, inner):
                turn[pl.ds(pl.multiple_of(i * 64, 64), 64), :] = turn_matrix(64, i * 64, False)
                return inner

            lax.fori_loop(0, ROWS // 64, tile, 0)

        @pl.when(j < 2)
        def _():
            fill(j + 1)

        @pl.when(j >= 1)
        def _():
            use_piece(j - 1)

        return carry

    lax.fori_loop(0, PIECES + 1, step, 0)

    def finish(i, carry):
        rows = pl.ds(pl.multiple_of(i * MSG, 16), MSG)
        g = acc[0, rows, :]
        act[rows, :] = (g / (1.0 + jnp.exp(-g)) * acc[1, rows, :]).astype(BF16)
        return carry

    lax.fori_loop(0, ROWS // MSG, finish, 0)

    for j in (PIECES - 2, PIECES - 1):
        sent(j)

    def sent_columns(j, carry):
        here = turned(j % 3)
        for n, o in enumerate(COLUMN):
            column_copy(n, j, j % 3, to_column(o, here), here[2] * 2 + here[3]).wait_send()
        return carry

    lax.fori_loop(0, PIECES, sent_columns, 0)


def dispatch(normed, table, w_gate, w_up):
    vmem = pl.BlockSpec(memory_space=pltpu.VMEM)
    hbm = pl.BlockSpec(memory_space=pltpu.HBM)
    dma = pltpu.SemaphoreType.DMA
    return pl.pallas_call(
        dispatch_kernel,
        name="dispatch",
        out_shape=[
            jax.ShapeDtypeStruct((ROWS, FF), BF16),
            jax.ShapeDtypeStruct((TYPES, 8, 2, PLANE, TOK), F32),
        ],
        in_specs=[hbm] * 4,
        out_specs=[vmem] * 2,
        scratch_shapes=[
            pltpu.VMEM((TOK, D), BF16),
            pltpu.VMEM((TYPES, 4, 2, PLANE, TOK), BF16),
            pltpu.VMEM((PIECES, 8 * TOK, PIECE), BF16),
            pltpu.VMEM((TYPES, 8, 2, PLANE, TOK), BF16),
            pltpu.VMEM((TYPES, ALL, 8 * TOK), BF16),
            pltpu.VMEM((2, ALL, PIECE), BF16),
            pltpu.VMEM((PIECES, 2, ROWS, PIECE), BF16),
            pltpu.VMEM((2, 2, 2, PIECE, FF), BF16),
            pltpu.VMEM((2, ROWS, FF), F32),
            pltpu.VMEM((320, 320), BF16),
            pltpu.VMEM((ROWS, ROWS), BF16),
            pltpu.VMEM((2, ROWS, PIECE), BF16),
            dma((2,)),
            dma((2, 2, 2)),
            dma((TYPES, len(COLUMN))),
            dma((TYPES, len(COLUMN))),
            dma((PIECES, len(COLUMN))),
            dma((PIECES, len(COLUMN))),
            dma((PIECES, len(OFFSETS))),
            dma((PIECES, len(OFFSETS))),
        ],
        compiler_params=pltpu.CompilerParams(
            collective_id=2, has_side_effects=True, vmem_limit_bytes=60 * 2**20
        ),
    )(normed, table, w_gate, w_up)


def combine_kernel(
    act_hbm, tables_hbm, w_down, hidden_hbm, out,
    acts, tables, wd, hidden, answers, got, mix, partial, sums, swap, turn,
    in_sem, msg_s, msg_r, col_s, col_r,
):
    loads = [
        pltpu.make_async_copy(act_hbm, acts.at[0], in_sem.at[0]),
        pltpu.make_async_copy(w_down, wd, in_sem.at[1]),
        pltpu.make_async_copy(tables_hbm, tables, in_sem.at[2]),
        pltpu.make_async_copy(hidden_hbm, hidden, in_sem.at[3]),
    ]
    for load in loads:
        load.start()
    greet_all()
    for load in loads:
        load.wait()

    def message(k, j, t, dev, src_dev):
        chip = dev[0] * 4 + dev[1]
        return pltpu.make_async_remote_copy(
            src_ref=answers.at[j % 3, dev[3], pl.ds(pl.multiple_of(chip * MSG, 16), MSG)],
            dst_ref=got.at[j, pl.ds(pl.multiple_of(plane_index(src_dev) * MSG, 16), MSG)],
            send_sem=msg_s.at[j, k], recv_sem=msg_r.at[j, k],
            device_id=turned_device(t, dev), device_id_type=MESH,
        )

    def column_copy(n, j, t, dev, src_dev):
        block = dev[2] * 2 + dev[3]
        return pltpu.make_async_remote_copy(
            src_ref=partial.at[j % 2, pl.ds(pl.multiple_of(block * TOK, TOK), TOK)],
            dst_ref=sums.at[j, src_dev[2], src_dev[3]],
            send_sem=col_s.at[j, n], recv_sem=col_r.at[j, n],
            device_id=turned_device(t, dev), device_id_type=MESH,
        )

    def sent(j):
        here = turned(j % 3)
        for k, o in enumerate(OFFSETS):
            message(k, j, j % 3, to_plane(o, here), here).wait_send()

    def sent_columns(j):
        here = turned(j % 3)
        for n, o in enumerate(COLUMN):
            column_copy(n, j, j % 3, to_column(o, here), here).wait_send()

    def send_piece(j):
        t = j % 3
        here = turned(t)
        for half in range(2):
            span = pl.ds(pl.multiple_of(half * HALF + j * PIECE, PIECE), PIECE)

            def tile(i, inner):
                rows = pl.ds(pl.multiple_of(i * (ROWS // 4), 16), ROWS // 4)
                answers[j % 3, half, rows, :] = jnp.dot(
                    acts[t, rows, :], wd[:, span], preferred_element_type=F32
                ).astype(BF16)
                return inner

            lax.fori_loop(0, 4, tile, 0)
        for k, o in enumerate(OFFSETS):
            message(k, j, t, to_plane(o, here), here).start()
        own_rows = pl.ds(pl.multiple_of(plane_index(here) * MSG, 16), MSG)
        own_place = pl.ds(pl.multiple_of((here[0] * 4 + here[1]) * MSG, 16), MSG)
        got[j, own_rows, :] = answers[j % 3, here[3], own_place, :]

    send_piece(0)
    swap[...] = swap_matrix()
    for i in range(4):
        rows = slice(i * 320, (i + 1) * 320)
        acts[1, rows, :] = jnp.dot(swap[...], acts[0, rows, :], preferred_element_type=F32).astype(BF16)
    send_piece(1)

    def turn_rows(i, carry):
        turn[...] = turn_matrix(64, i * 64, True)
        acts[2, pl.ds(pl.multiple_of(i * 64, 64), 64), :] = jnp.dot(
            turn[...], acts[0], preferred_element_type=F32
        ).astype(BF16)
        return carry

    lax.fori_loop(0, ROWS // 64, turn_rows, 0)
    send_piece(2)

    block, place = table_rows()

    def fill(i, carry):
        t = i // 4
        p = i % 4
        for b in range(8):
            rows = []
            for n in range(8):
                l = p * 8 + n
                hit = (tables[t, b, 0, pl.ds(l, 1), :] == place) & (block == b)
                rows.append(jnp.where(hit, tables[t, b, 1, pl.ds(l, 1), :], 0.0))
            whole = jnp.concatenate(rows, axis=0)
            mix[t, b * TOK : (b + 1) * TOK, pl.ds(pl.multiple_of(p * 8 * MSG, TOK), 8 * MSG)] = whole.T.astype(BF16)
        return carry

    lax.fori_loop(0, TYPES * PLANE // 8, fill, 0)

    def reduce_piece(j):
        t = j % 3
        here = turned(t)
        for k, o in enumerate(OFFSETS):
            message(k, j, t, here, from_plane(o, here)).wait_recv()

        @pl.when(j >= 2)
        def _():
            sent_columns(j - 2)

        def tile(i, carry):
            rows = pl.ds(pl.multiple_of(i * 256, 256), 256)
            partial[j % 2, rows, :] = jnp.dot(mix[t, rows, :], got[j], preferred_element_type=F32).astype(BF16)
            return carry

        lax.fori_loop(0, 4, tile, 0)
        for n, o in enumerate(COLUMN):
            column_copy(n, j, t, to_column(o, here), here).start()
        me = here[2] * 2 + here[3]
        sums[j, here[2], here[3]] = partial[j % 2, pl.ds(pl.multiple_of(me * TOK, TOK), TOK), :]

    def finish_piece(j):
        t = j % 3
        here = turned(t)
        for n, o in enumerate(COLUMN):
            column_copy(n, j, t, here, from_column(o, here)).wait_recv()
        for half in range(2):
            span = pl.ds(pl.multiple_of(half * HALF + j * PIECE, PIECE), PIECE)
            total = hidden[:, span]
            for n in range(4):
                total = total + sums[j, n, half].astype(F32)
            out[:, span] = total.astype(BF16)

    def step(j, carry):
        @pl.when(j < PIECES)
        def _():
            reduce_piece(j)

        @pl.when(j < PIECES - 3)
        def _():
            sent(j)
            send_piece(j + 3)

        @pl.when(j >= 1)
        def _():
            finish_piece(j - 1)

        return carry

    lax.fori_loop(0, PIECES + 1, step, 0)

    for j in range(PIECES - 3, PIECES):
        sent(j)
    for j in range(PIECES - 2, PIECES):
        sent_columns(j)


def combine(act, tables, w_down, hidden):
    hbm = pl.BlockSpec(memory_space=pltpu.HBM)
    dma = pltpu.SemaphoreType.DMA
    return pl.pallas_call(
        combine_kernel,
        name="combine",
        out_shape=jax.ShapeDtypeStruct((TOK, D), BF16),
        in_specs=[hbm] * 4,
        out_specs=pl.BlockSpec(memory_space=pltpu.VMEM),
        scratch_shapes=[
            pltpu.VMEM((TYPES, ROWS, FF), BF16),
            pltpu.VMEM((TYPES, 8, 2, PLANE, TOK), F32),
            pltpu.VMEM((FF, D), BF16),
            pltpu.VMEM((TOK, D), F32),
            pltpu.VMEM((3, 2, ROWS, PIECE), BF16),
            pltpu.VMEM((PIECES, ALL, PIECE), BF16),
            pltpu.VMEM((TYPES, 8 * TOK, ALL), BF16),
            pltpu.VMEM((2, 8 * TOK, PIECE), BF16),
            pltpu.VMEM((PIECES, 4, 2, TOK, PIECE), BF16),
            pltpu.VMEM((320, 320), BF16),
            pltpu.VMEM((64, ROWS), BF16),
            dma((4,)),
            dma((PIECES, len(OFFSETS))),
            dma((PIECES, len(OFFSETS))),
            dma((PIECES, len(COLUMN))),
            dma((PIECES, len(COLUMN))),
        ],
        compiler_params=pltpu.CompilerParams(
            collective_id=3, has_side_effects=True, vmem_limit_bytes=60 * 2**20
        ),
    )(act, tables, w_down, hidden)


def body(
    queries, fresh_keys, fresh_values, stored_keys, stored_values, column_blocks, diagonal_offsets,
    residual, norm_gain, routes, gate_weights, w_gate, w_up, w_down,
):
    kv = exchange(*collect(column_blocks, diagonal_offsets, stored_keys, stored_values))
    hidden, normed, table = attend(
        column_blocks, diagonal_offsets, queries, fresh_keys, fresh_values, kv,
        residual, norm_gain, routes, gate_weights,
    )
    act, tables = dispatch(normed, table, w_gate[0], w_up[0])
    return combine(act, tables, w_down[0], hidden)


def solution(mesh):
    rows = P(("ctx", "exp"), None)
    experts = P(("ctx", "exp"), None, None)
    in_specs = (
        rows, rows, rows, P("ctx", None), P("ctx", None), P(), P(), rows, P(), rows, rows,
        experts, experts, experts,
    )
    return jax.shard_map(body, mesh=mesh, in_specs=in_specs, out_specs=rows, check_vma=False)
```

```python
import functools

import jax
import jax.numpy as jnp
from jax import lax
from jax.experimental import pallas as pl
from jax.experimental.pallas import tpu as pltpu
from jax.sharding import PartitionSpec as P

MESH = pl.DeviceIdType.MESH
BF16 = jnp.bfloat16
F32 = jnp.float32
BLOCK = 64
HEAD = 128
HEADS_KV = 2
GROUP = 16
VERT = 2
SLASH = 8
SLOTS = VERT + 2 * SLASH
TOK = 128
D = 4096
FF = 768
HALF = D // 2
CAP = 10
PLANE = 32
MSG = 8 * CAP
ROWS = 16 * MSG
ALL = PLANE * MSG
PIECE = 256
PIECES = HALF // PIECE
NEG = -1e30


STAGED = 5
AHEAD = 4
ANSWERED = 4
TYPES = 3


def coords():
    ctx = lax.axis_index("ctx")
    exp = lax.axis_index("exp")
    return ((exp // 4) % 2) * 2 + ctx // 2, exp % 4, exp // 8, ctx % 2


def device(x, y, z, c):
    return ((x % 2) * 2 + c, z * 8 + (x // 2) * 4 + y)


def unit(t):
    return (2 - t) * (1 - t) // 2, t * (2 - t), t * (t - 1) // 2


def turned(t):
    x, y, z, c = coords()
    t0, t1, t2 = unit(t)
    return x * (t0 + t1) + y * t2, y * t0 + z * (t1 + t2), z * t0 + y * t1 + x * t2, c


def turned_device(t, dev):
    p, q, a, c = dev
    t0, t1, t2 = unit(t)
    return device(p * (t0 + t1) + a * t2, q * t0 + a * t1 + p * t2, a * t0 + q * (t1 + t2), c)


def plane_index(dev):
    return (dev[0] * 4 + dev[1]) * 2 + dev[3]


def ordered_offsets():
    left = [(dx, dy, dc) for dx in range(4) for dy in range(4) for dc in range(2) if dx or dy or dc]
    use = {}
    out = []

    def links(o):
        found = []
        for axis in range(2):
            if o[axis] == 1:
                found.append((axis, 1))
            elif o[axis] == 3:
                found.append((axis, -1))
            elif o[axis] == 2:
                found += [(axis, 1), (axis, -1)]
        return found

    while left:
        best = min(left, key=lambda o: (sum(2 * use.get(k, 0) + 1 for k in links(o)), -len(links(o)), o))
        left.remove(best)
        out.append(best)
        for k in links(best):
            use[k] = use.get(k, 0) + 1
    return out


OFFSETS = ordered_offsets()
COLUMN = [(1, 0), (3, 1), (2, 0), (3, 0), (1, 1), (2, 1), (0, 1)]
PEERS = [
    (dx, dy, dz, dc)
    for dx in range(4)
    for dy in range(4)
    for dz in range(4)
    for dc in range(2)
    if dx * dy * dz == 0 and (dx or dy or dz or dc)
]


def to_plane(o, dev):
    return (dev[0] + o[0]) % 4, (dev[1] + o[1]) % 4, dev[2], (dev[3] + o[2]) % 2


def from_plane(o, dev):
    return (dev[0] + 4 - o[0]) % 4, (dev[1] + 4 - o[1]) % 4, dev[2], (dev[3] + 2 - o[2]) % 2


def to_column(o, dev):
    return dev[0], dev[1], (dev[2] + o[0]) % 4, (dev[3] + o[1]) % 2


def from_column(o, dev):
    return dev[0], dev[1], (dev[2] + 4 - o[0]) % 4, (dev[3] + 2 - o[1]) % 2


CUTS = (0, 11, 21, 31)


def roll(start, step):
    kinds = [(step + 3 - i) % 3 for i in range(3)]
    places = [turned(t) for t in kinds]
    steady = (step >= 2) & (step < PIECES)

    @pl.when(steady)
    def _():
        for n in range(CUTS[1]):
            for i in range(3):
                if CUTS[i] + n < CUTS[i + 1]:
                    start(CUTS[i] + n, step - i, kinds[i], places[i])

    for i in range(3):

        @pl.when(jnp.logical_not(steady) & (step >= i) & (step - i < PIECES))
        def _():
            for k in range(CUTS[i], CUTS[i + 1]):
                start(k, step - i, kinds[i], places[i])


def greet_all():
    bar = pltpu.get_barrier_semaphore()
    x, y, z, c = coords()
    for o in PEERS:
        other = device((x + o[0]) % 4, (y + o[1]) % 4, (z + o[2]) % 4, (c + o[3]) % 2)
        pl.semaphore_signal(bar, inc=1, device_id=other, device_id_type=MESH)
    pl.semaphore_wait(bar, len(PEERS))


def digits(row):
    n = (row * 3277) >> 16
    return n >> 4, (n >> 2) & 3, n & 3, row - n * 20


def swap_matrix():
    row = lax.broadcasted_iota(jnp.int32, (320, 1), 0)
    _, d2, d1, rest = digits(row)
    source = d1 * 80 + d2 * 20 + rest
    return (lax.broadcasted_iota(jnp.int32, (320, 320), 1) == source).astype(F32).astype(BF16)


def turn_matrix(rows, start, back):
    row = lax.broadcasted_iota(jnp.int32, (rows, 1), 0) + start
    d3, d2, d1, rest = digits(row)
    source = d1 * 320 + d3 * 80 + d2 * 20 + rest if back else d2 * 320 + d1 * 80 + d3 * 20 + rest
    return (lax.broadcasted_iota(jnp.int32, (rows, ROWS), 1) == source).astype(F32).astype(BF16)


def side(h):
    exp = lax.axis_index("exp")
    return exp + h * (4 - 8 * ((exp // 4) % 2))


def collect_kernel(cols, offs, keys_hbm, values_hbm, con, near, keys, values, sem):
    loads = [pltpu.make_async_copy(keys_hbm, keys, sem.at[0]), pltpu.make_async_copy(values_hbm, values, sem.at[1])]
    for load in loads:
        load.start()
    ctx = lax.axis_index("ctx")
    xl = ctx // 2
    for load in loads:
        load.wait()

    def put(h, slot, block_a, block_b):
        near_a = block_a - 32 * ctx
        near_b = block_b - 32 * ctx
        local = jnp.where((near_a >= 0) & (near_a < 32), near_a, near_b)
        inside = (local >= 0) & (local < 32)
        start = pl.multiple_of(jnp.clip(local, 0, 31) * BLOCK, BLOCK)
        factor = jnp.where(inside, 1.0, 0.0).astype(BF16)
        for kind, ref in ((0, keys), (1, values)):
            block = ref[pl.ds(start, BLOCK), h * HEAD : (h + 1) * HEAD]
            con[kind, h, slot * BLOCK : (slot + 1) * BLOCK, :] = block * factor

    for h in range(HEADS_KV):
        exp = jnp.where(xl == 0, side(h), side(0))
        for v in range(VERT):
            put(h, v, cols[h, v], cols[h, v])
            here = (cols[h, v] // 64) == xl
            near[h * SLOTS + v] = jnp.full((8, HEAD), jnp.where(here, 1.0, 0.0), F32)
        for i in range(2):
            for s in range(SLASH):
                block_2 = 256 + 2 * exp + i - offs[h, s]
                slot = VERT + i * SLASH + s
                put(h, slot, block_2, block_2 + 64)
                near[h * SLOTS + slot] = jnp.full((8, HEAD), jnp.where(block_2 >= 0, 1.0, 0.0), F32)


def collect(cols, offs, keys, values):
    return pl.pallas_call(
        collect_kernel,
        name="collect_blocks",
        out_shape=[
            jax.ShapeDtypeStruct((2, HEADS_KV, SLOTS * BLOCK, HEAD), BF16),
            jax.ShapeDtypeStruct((HEADS_KV * SLOTS, 8, HEAD), F32),
        ],
        in_specs=[pl.BlockSpec(memory_space=pltpu.SMEM)] * 2 + [pl.BlockSpec(memory_space=pltpu.HBM)] * 2,
        out_specs=[pl.BlockSpec(memory_space=pltpu.VMEM)] * 2,
        scratch_shapes=[
            pltpu.VMEM((2048, HEADS_KV * HEAD), BF16),
            pltpu.VMEM((2048, HEADS_KV * HEAD), BF16),
            pltpu.SemaphoreType.DMA((2,)),
        ],
        compiler_params=pltpu.CompilerParams(vmem_limit_bytes=16 * 2**20),
    )(cols, offs, keys, values)


def exchange_kernel(con, near, out, sib, chip, rem, fin, arr, ssem, rsem):
    x, y, z, c = coords()
    xl = x % 2
    exp = lax.axis_index("exp")
    twin = (xl * 2 + 1 - c, exp)
    across = [((1 - xl) * 2 + c, side(h)) for h in range(HEADS_KV)]
    bar = pltpu.get_barrier_semaphore()
    for other in (twin, *across):
        pl.semaphore_signal(bar, inc=1, device_id=other, device_id_type=MESH)
    pl.semaphore_wait(bar, 3)

    first = pltpu.make_async_remote_copy(
        src_ref=con.at[1 - c], dst_ref=sib, send_sem=ssem.at[0], recv_sem=rsem.at[0],
        device_id=twin, device_id_type=MESH,
    )
    first.start()
    first.wait()
    chip[...] = con[c] + sib[...]

    verts = VERT * BLOCK

    def whole(h):
        return pltpu.make_async_remote_copy(
            src_ref=chip.at[h], dst_ref=rem.at[h], send_sem=ssem.at[1 + h], recv_sem=rsem.at[1 + h],
            device_id=across[h], device_id_type=MESH,
        )

    def vertical(h):
        return pltpu.make_async_remote_copy(
            src_ref=chip.at[h, pl.ds(0, verts)], dst_ref=rem.at[h, pl.ds(0, verts)],
            send_sem=ssem.at[1 + h], recv_sem=rsem.at[1 + h],
            device_id=across[h], device_id_type=MESH,
        )

    @pl.when(xl == 0)
    def _():
        for h in range(HEADS_KV):
            whole(h).start()

    @pl.when(xl == 1)
    def _():
        for h in range(HEADS_KV):
            vertical(h).start()

    def back(h):
        return pltpu.make_async_remote_copy(
            src_ref=fin.at[h], dst_ref=arr.at[h], send_sem=ssem.at[3 + h], recv_sem=rsem.at[3 + h],
            device_id=twin, device_id_type=MESH,
        )

    def pick(h, slot):
        span = slice(slot * BLOCK, (slot + 1) * BLOCK)
        local = near[h * SLOTS + slot, 0:1, :].astype(BF16)
        far = rem[h, span, :]
        return span, chip[h, span, :] * local + far * (1.0 - local).astype(BF16), far

    def pick_verticals(h):
        for v in range(VERT):
            span, mixed, _ = pick(h, v)
            fin[h, span, :] = mixed
            out[c, h, span, :] = mixed

    for h in range(HEADS_KV):

        @pl.when(xl == 0)
        def _():
            vertical(h).wait_recv()
            pick_verticals(h)
            fin[h, verts:, :] = jnp.zeros((2 * SLASH * BLOCK, HEAD), BF16)
            out[c, h, verts:, :] = jnp.zeros((2 * SLASH * BLOCK, HEAD), BF16)

        @pl.when(xl == 1)
        def _():
            whole(h).wait_recv()
            pick_verticals(h)
            for slot in range(VERT, SLOTS):
                span, mixed, far = pick(h, slot)

                @pl.when(c == 1)
                def _():
                    out[1, h, span, :] = mixed
                    fin[h, span, :] = far

                @pl.when(c == 0)
                def _():
                    out[0, h, span, :] = far
                    fin[h, span, :] = mixed

        back(h).start()

    for h in range(HEADS_KV):
        back(h).wait()
        out[1 - c, h] = arr[h]

    @pl.when(xl == 0)
    def _():
        for h in range(HEADS_KV):
            whole(h).wait_send()

    @pl.when(xl == 1)
    def _():
        for h in range(HEADS_KV):
            vertical(h).wait_send()


def exchange(con, near):
    part = (HEADS_KV, SLOTS * BLOCK, HEAD)
    return pl.pallas_call(
        exchange_kernel,
        name="key_exchange",
        out_shape=jax.ShapeDtypeStruct((2,) + part, BF16),
        in_specs=[pl.BlockSpec(memory_space=pltpu.VMEM)] * 2,
        out_specs=pl.BlockSpec(memory_space=pltpu.VMEM),
        scratch_shapes=[
            pltpu.VMEM(part, BF16),
            pltpu.VMEM(part, BF16),
            pltpu.VMEM(part, BF16),
            pltpu.VMEM(part, BF16),
            pltpu.VMEM(part, BF16),
            pltpu.SemaphoreType.DMA((5,)),
            pltpu.SemaphoreType.DMA((5,)),
        ],
        compiler_params=pltpu.CompilerParams(
            collective_id=1, has_side_effects=True, vmem_limit_bytes=24 * 2**20
        ),
    )(con, near)


def attend_kernel(
    cols, offs, q, fk, fv, kv, res, gain, routes, gates, hidden_out, normed_out, table_out,
    hidden, normed, table, sem,
):
    puts = []

    def put(src, dst):
        copy = pltpu.make_async_copy(src, dst, sem.at[len(puts)])
        copy.start()
        puts.append(copy)

    ctx = lax.axis_index("ctx")
    exp = lax.axis_index("exp")

    ids = routes[...]
    group, rest = ids >> 5, ids & 31
    ex, ey, ez, ec = ((rest >> 2) & 1) * 2 + (group >> 1), rest & 3, rest >> 3, group & 1
    lanes = lax.broadcasted_iota(jnp.int32, (TOK, TOK), 1)
    subs = lax.broadcasted_iota(jnp.int32, (TOK, TOK), 0)
    later = (subs < lanes).astype(F32).astype(BF16)
    for t, (p, r, a) in enumerate(((ex, ey, ez), (ex, ez, ey), (ey, ez, ex))):
        number = a * PLANE + (p * 4 + r) * 2 + ec
        named = jnp.zeros((TOK, TOK), F32)
        strength = jnp.zeros((TOK, TOK), F32)
        for n in range(8):
            hit = number[n : n + 1, :] == subs
            named = named + jnp.where(hit, 1.0, 0.0)
            strength = strength + jnp.where(hit, gates[n : n + 1, :], 0.0)
        place = jnp.dot(named.astype(BF16), later, preferred_element_type=F32)
        place = jnp.where(named > 0.5, place, -1.0).astype(BF16)
        strength = strength.astype(BF16)
        for n in range(4):
            table[t, n, 0] = place[n * PLANE : (n + 1) * PLANE]
            table[t, n, 1] = strength[n * PLANE : (n + 1) * PLANE]
    put(table, table_out)

    scale = 1.0 / HEAD**0.5
    lane = lax.broadcasted_iota(jnp.int32, (1, (VERT + SLASH) * BLOCK), 1) // BLOCK
    heads = 4
    ones = jnp.ones(((VERT + SLASH) * BLOCK, HEAD), BF16)
    for h in range(HEADS_KV):
        for i in range(2):
            block = 128 + 2 * (ctx * 32 + exp) + i
            listed = [cols[h, v] for v in range(VERT)] + [block - offs[h, s] for s in range(SLASH)]
            bias = jnp.zeros(lane.shape, F32)
            for n, one in enumerate(listed):
                kept = (one >= 0) & (one < 128)
                for before in listed[:n]:
                    kept = kept & (one != before)
                bias = jnp.where(lane == n, jnp.where(kept, 0.0, NEG), bias)
            slash = VERT * BLOCK + i * SLASH * BLOCK
            k = jnp.concatenate([kv[0, h, : VERT * BLOCK, :], kv[0, h, slash : slash + SLASH * BLOCK, :]], axis=0)
            v = jnp.concatenate([kv[1, h, : VERT * BLOCK, :], kv[1, h, slash : slash + SLASH * BLOCK, :]], axis=0)
            v = jnp.concatenate([v, ones], axis=1)
            rows = slice(i * BLOCK, (i + 1) * BLOCK)
            own_k = fk[rows, h * HEAD : (h + 1) * HEAD].astype(F32)
            own_v = fv[rows, h * HEAD : (h + 1) * HEAD].astype(F32)
            own_k = jnp.concatenate([own_k] * heads, axis=0)
            own_v = jnp.concatenate([own_v] * heads, axis=0)
            for g in range(0, GROUP, heads):
                spans = [slice((h * GROUP + g + n) * HEAD, (h * GROUP + g + n + 1) * HEAD) for n in range(heads)]
                part = jnp.concatenate([q[rows, span] for span in spans], axis=0)
                scores = lax.dot_general(part, k, (((1,), (1,)), ((), ())), preferred_element_type=F32)
                scores = scores * scale + bias
                own = jnp.sum(part.astype(F32) * own_k, axis=1, keepdims=True) * scale
                top = jnp.maximum(own, jnp.max(scores, axis=1, keepdims=True))
                weights = jnp.exp(scores - top).astype(BF16)
                own_weight = jnp.exp(own - top).astype(BF16).astype(F32)
                both = jnp.dot(weights, v, preferred_element_type=F32)
                numer = both[:, :HEAD] + own_weight * own_v
                denom = both[:, HEAD:] + own_weight
                attended = numer / denom
                for n, span in enumerate(spans):
                    hidden[rows, span] = res[rows, span].astype(F32) + attended[n * BLOCK : (n + 1) * BLOCK]
            done = hidden.at[pl.ds(i * BLOCK, BLOCK), pl.ds(h * GROUP * HEAD, GROUP * HEAD)]
            put(done, hidden_out.at[pl.ds(i * BLOCK, BLOCK), pl.ds(h * GROUP * HEAD, GROUP * HEAD)])

    for r in range(0, TOK, 16):
        part = hidden[r : r + 16, :]
        spread = jnp.mean(part * part, axis=1, keepdims=True)
        normed[r : r + 16, :] = (part * lax.rsqrt(spread + 1e-6) * gain[...]).astype(BF16)

    put(normed, normed_out)
    for copy in puts:
        copy.wait()


def attend(cols, offs, q, fk, fv, kv, res, gain, routes, gates):
    vmem = pl.BlockSpec(memory_space=pltpu.VMEM)
    shapes = [((TOK, D), F32), ((TOK, D), BF16), ((TYPES, 4, 2, PLANE, TOK), BF16)]
    return pl.pallas_call(
        attend_kernel,
        name="attention",
        out_shape=[jax.ShapeDtypeStruct(*one) for one in shapes],
        in_specs=[pl.BlockSpec(memory_space=pltpu.SMEM)] * 2 + [vmem] * 8,
        out_specs=[pl.BlockSpec(memory_space=pltpu.HBM)] * 3,
        scratch_shapes=[pltpu.VMEM(*one) for one in shapes] + [pltpu.SemaphoreType.DMA((6,))],
        compiler_params=pltpu.CompilerParams(vmem_limit_bytes=32 * 2**20),
    )(cols, offs, q, fk, fv, kv, res, gain.reshape(1, D), routes.T, gates.T)


def table_rows():
    row = lax.broadcasted_iota(jnp.int32, (MSG, TOK), 0)
    block = jnp.zeros((MSG, TOK), jnp.int32)
    for b in range(1, 8):
        block = block + jnp.where(row >= b * CAP, 1, 0)
    return block, (row - block * CAP).astype(F32)


def dispatch_kernel(
    normed_hbm, table_hbm, w_gate, w_up, act, tables_out,
    normed, table, x_all, tables, select, stage, got, weights, acc, swap, turn, sorted_rows,
    in_sem, w_sem, tab_s, tab_r, col_s, col_r, msg_s, msg_r,
):
    loads = [
        pltpu.make_async_copy(table_hbm, table, in_sem.at[0]),
        pltpu.make_async_copy(normed_hbm, normed, in_sem.at[1]),
    ]
    for load in loads:
        load.start()

    def weight_loads(j):
        return [
            pltpu.make_async_copy(
                w.at[pl.ds(pl.multiple_of(half * HALF + j * PIECE, PIECE), PIECE)],
                weights.at[j % 2, n, half],
                w_sem.at[j % 2, n, half],
            )
            for n, w in enumerate((w_gate, w_up))
            for half in range(2)
        ]

    for j in range(2):
        for load in weight_loads(j):
            load.start()
    greet_all()
    for load in loads:
        load.wait()

    def table_copy(n, t, dev, slot):
        return pltpu.make_async_remote_copy(
            src_ref=table.at[t, dev[2]], dst_ref=tables.at[t, slot], send_sem=tab_s.at[t, n], recv_sem=tab_r.at[t, n],
            device_id=turned_device(t, dev), device_id_type=MESH,
        )

    def column_copy(n, j, t, dev, slot):
        start = pl.multiple_of(dev[3] * HALF + j * PIECE, PIECE)
        return pltpu.make_async_remote_copy(
            src_ref=normed.at[:, pl.ds(start, PIECE)],
            dst_ref=x_all.at[j, pl.ds(pl.multiple_of(slot * TOK, TOK), TOK)],
            send_sem=col_s.at[j, n], recv_sem=col_r.at[j, n],
            device_id=turned_device(t, dev), device_id_type=MESH,
        )

    for t in range(TYPES):
        here = turned(t)
        me = here[2] * 2 + here[3]
        for n, o in enumerate(COLUMN):
            table_copy(n, t, to_column(o, here), me).start()
        tables[t, me] = table[t, here[2]]

    def send_columns(j, carry):
        t = j % 3
        here = turned(t)
        me = here[2] * 2 + here[3]
        for n, o in enumerate(COLUMN):
            column_copy(n, j, t, to_column(o, here), me).start()
        start = pl.multiple_of(here[3] * HALF + j * PIECE, PIECE)
        x_all[j, pl.ds(pl.multiple_of(me * TOK, TOK), TOK), :] = normed[:, pl.ds(start, PIECE)]
        return carry

    lax.fori_loop(0, PIECES, send_columns, 0)

    for t in range(TYPES):
        here = turned(t)
        for n, o in enumerate(COLUMN):
            dev = from_column(o, here)
            table_copy(n, t, dev, dev[2] * 2 + dev[3]).wait()
    tables_out[...] = tables[...].astype(F32)

    block, place = table_rows()

    def fill(t):
        def one(l, carry):
            for b in range(8):
                row = tables_out[t, b, 0, pl.ds(l, 1), :]
                hit = (row == place) & (block == b)
                select[t, pl.ds(pl.multiple_of(l * MSG, 16), MSG), b * TOK : (b + 1) * TOK] = jnp.where(
                    hit, 1.0, 0.0
                ).astype(BF16)
            return carry

        lax.fori_loop(0, PLANE, one, 0)

    fill(0)

    def message(k, j, t, dev, src_dev):
        chip = src_dev[0] * 4 + src_dev[1]
        return pltpu.make_async_remote_copy(
            src_ref=stage.at[j % STAGED, pl.ds(pl.multiple_of(plane_index(dev) * MSG, 16), MSG)],
            dst_ref=got.at[j, src_dev[3], pl.ds(pl.multiple_of(chip * MSG, 16), MSG)],
            send_sem=msg_s.at[j, k], recv_sem=msg_r.at[j, k],
            device_id=turned_device(t, dev), device_id_type=MESH,
        )

    def sent(j):
        here = turned(j % 3)
        for k, o in enumerate(OFFSETS):
            message(k, j, j % 3, to_plane(o, here), here).wait_send()

    def send_piece(j):
        t = j % 3
        here = turned(t)
        for n, o in enumerate(COLUMN):
            dev = from_column(o, here)
            column_copy(n, j, t, dev, dev[2] * 2 + dev[3]).wait_recv()

        @pl.when(j >= STAGED)
        def _():
            sent(j - STAGED)

        step = ALL // 8

        def tile(i, carry):
            rows = pl.ds(pl.multiple_of(i * step, 16), step)
            stage[j % STAGED, rows, :] = jnp.dot(select[t, rows, :], x_all[j], preferred_element_type=F32).astype(BF16)
            return carry

        lax.fori_loop(0, 8, tile, 0)
        own_rows = pl.ds(pl.multiple_of(plane_index(here) * MSG, 16), MSG)
        own_place = pl.ds(pl.multiple_of((here[0] * 4 + here[1]) * MSG, 16), MSG)
        got[j, here[3], own_place, :] = stage[j % STAGED, own_rows, :]

    def start(k, j, t, here):
        message(k, j, t, to_plane(OFFSETS[k], here), here).start()

    def use_piece(j):
        t = j % 3
        here = turned(t)
        for load in weight_loads(j):
            load.wait()
        for k, o in enumerate(OFFSETS):
            message(k, j, t, here, from_plane(o, here)).wait_recv()

        @pl.when(t == 0)
        def _():
            sorted_rows[...] = got[j]

        @pl.when(t == 1)
        def _():
            for half in range(2):
                for i in range(4):
                    rows = slice(i * 320, (i + 1) * 320)
                    sorted_rows[half, rows, :] = jnp.dot(
                        swap[...], got[j, half, rows, :], preferred_element_type=F32
                    ).astype(BF16)

        @pl.when(t == 2)
        def _():
            def tile(i, carry):
                rows = pl.ds(pl.multiple_of(i * 320, 16), 320)
                turn[...] = turn_matrix(320, i * 320, False)
                for half in range(2):
                    sorted_rows[half, rows, :] = jnp.dot(
                        turn[...], got[j, half], preferred_element_type=F32
                    ).astype(BF16)
                return carry

            lax.fori_loop(0, 4, tile, 0)

        step = ROWS // 5

        def tile(i, carry):
            rows = pl.ds(pl.multiple_of(i * step, 16), step)
            left = sorted_rows[0, rows, :]
            right = sorted_rows[1, rows, :]
            for n in range(2):
                acc[n, rows, :] += jnp.dot(left, weights[j % 2, n, 0], preferred_element_type=F32) + jnp.dot(
                    right, weights[j % 2, n, 1], preferred_element_type=F32
                )
            return carry

        lax.fori_loop(0, 5, tile, 0)

        @pl.when(j + 2 < PIECES)
        def _():
            for load in weight_loads(j + 2):
                load.start()

    def step(j, carry):
        @pl.when(j < PIECES)
        def _():
            send_piece(j)

        roll(start, j)

        @pl.when(j == 0)
        def _():
            acc[...] = jnp.zeros_like(acc)
            swap[...] = swap_matrix()

        @pl.when(j < 2)
        def _():
            fill(j + 1)

        @pl.when(j >= AHEAD)
        def _():
            use_piece(j - AHEAD)

        return carry

    lax.fori_loop(0, PIECES + AHEAD, step, 0)

    def finish(i, carry):
        rows = pl.ds(pl.multiple_of(i * MSG, 16), MSG)
        g = acc[0, rows, :]
        act[rows, :] = (g / (1.0 + jnp.exp(-g)) * acc[1, rows, :]).astype(BF16)
        return carry

    lax.fori_loop(0, ROWS // MSG, finish, 0)

    for j in range(PIECES - STAGED, PIECES):
        sent(j)

    def sent_columns(j, carry):
        here = turned(j % 3)
        for n, o in enumerate(COLUMN):
            column_copy(n, j, j % 3, to_column(o, here), here[2] * 2 + here[3]).wait_send()
        return carry

    lax.fori_loop(0, PIECES, sent_columns, 0)


def dispatch(normed, table, w_gate, w_up):
    vmem = pl.BlockSpec(memory_space=pltpu.VMEM)
    hbm = pl.BlockSpec(memory_space=pltpu.HBM)
    dma = pltpu.SemaphoreType.DMA
    return pl.pallas_call(
        dispatch_kernel,
        name="dispatch",
        out_shape=[
            jax.ShapeDtypeStruct((ROWS, FF), BF16),
            jax.ShapeDtypeStruct((TYPES, 8, 2, PLANE, TOK), F32),
        ],
        in_specs=[hbm] * 4,
        out_specs=[vmem] * 2,
        scratch_shapes=[
            pltpu.VMEM((TOK, D), BF16),
            pltpu.VMEM((TYPES, 4, 2, PLANE, TOK), BF16),
            pltpu.VMEM((PIECES, 8 * TOK, PIECE), BF16),
            pltpu.VMEM((TYPES, 8, 2, PLANE, TOK), BF16),
            pltpu.VMEM((TYPES, ALL, 8 * TOK), BF16),
            pltpu.VMEM((STAGED, ALL, PIECE), BF16),
            pltpu.VMEM((PIECES, 2, ROWS, PIECE), BF16),
            pltpu.VMEM((2, 2, 2, PIECE, FF), BF16),
            pltpu.VMEM((2, ROWS, FF), F32),
            pltpu.VMEM((320, 320), BF16),
            pltpu.VMEM((320, ROWS), BF16),
            pltpu.VMEM((2, ROWS, PIECE), BF16),
            dma((2,)),
            dma((2, 2, 2)),
            dma((TYPES, len(COLUMN))),
            dma((TYPES, len(COLUMN))),
            dma((PIECES, len(COLUMN))),
            dma((PIECES, len(COLUMN))),
            dma((PIECES, len(OFFSETS))),
            dma((PIECES, len(OFFSETS))),
        ],
        compiler_params=pltpu.CompilerParams(
            collective_id=2, has_side_effects=True, vmem_limit_bytes=62 * 2**20
        ),
    )(normed, table, w_gate, w_up)


def combine_kernel(
    act_hbm, tables_hbm, w_down, hidden_hbm, out,
    acts, tables, wd, hidden, answers, got, mix, partial, sums, swap, turn,
    in_sem, msg_s, msg_r, col_s, col_r,
):
    loads = [
        pltpu.make_async_copy(act_hbm, acts.at[0], in_sem.at[0]),
        pltpu.make_async_copy(w_down, wd, in_sem.at[1]),
        pltpu.make_async_copy(tables_hbm, tables, in_sem.at[2]),
        pltpu.make_async_copy(hidden_hbm, hidden, in_sem.at[3]),
    ]
    for load in loads:
        load.start()
    greet_all()
    for load in loads:
        load.wait()

    def message(k, j, t, dev, src_dev):
        chip = dev[0] * 4 + dev[1]
        return pltpu.make_async_remote_copy(
            src_ref=answers.at[j % ANSWERED, dev[3], pl.ds(pl.multiple_of(chip * MSG, 16), MSG)],
            dst_ref=got.at[j, pl.ds(pl.multiple_of(plane_index(src_dev) * MSG, 16), MSG)],
            send_sem=msg_s.at[j, k], recv_sem=msg_r.at[j, k],
            device_id=turned_device(t, dev), device_id_type=MESH,
        )

    def column_copy(n, j, t, dev, src_dev):
        block = dev[2] * 2 + dev[3]
        return pltpu.make_async_remote_copy(
            src_ref=partial.at[j % 2, pl.ds(pl.multiple_of(block * TOK, TOK), TOK)],
            dst_ref=sums.at[j, src_dev[2], src_dev[3]],
            send_sem=col_s.at[j, n], recv_sem=col_r.at[j, n],
            device_id=turned_device(t, dev), device_id_type=MESH,
        )

    def sent(j):
        here = turned(j % 3)
        for k, o in enumerate(OFFSETS):
            message(k, j, j % 3, to_plane(o, here), here).wait_send()

    def sent_columns(j):
        here = turned(j % 3)
        for n, o in enumerate(COLUMN):
            column_copy(n, j, j % 3, to_column(o, here), here).wait_send()

    def send_piece(j):
        t = j % 3
        here = turned(t)
        for half in range(2):
            span = pl.ds(pl.multiple_of(half * HALF + j * PIECE, PIECE), PIECE)

            def tile(i, inner):
                rows = pl.ds(pl.multiple_of(i * (ROWS // 4), 16), ROWS // 4)
                answers[j % ANSWERED, half, rows, :] = jnp.dot(
                    acts[t, rows, :], wd[:, span], preferred_element_type=F32
                ).astype(BF16)
                return inner

            lax.fori_loop(0, 4, tile, 0)
        own_rows = pl.ds(pl.multiple_of(plane_index(here) * MSG, 16), MSG)
        own_place = pl.ds(pl.multiple_of((here[0] * 4 + here[1]) * MSG, 16), MSG)
        got[j, own_rows, :] = answers[j % ANSWERED, here[3], own_place, :]
        for k, o in enumerate(OFFSETS):
            message(k, j, t, to_plane(o, here), here).start()

    send_piece(0)
    swap[...] = swap_matrix()
    for i in range(4):
        rows = slice(i * 320, (i + 1) * 320)
        acts[1, rows, :] = jnp.dot(swap[...], acts[0, rows, :], preferred_element_type=F32).astype(BF16)
    send_piece(1)

    def turn_rows(i, carry):
        turn[...] = turn_matrix(64, i * 64, True)
        acts[2, pl.ds(pl.multiple_of(i * 64, 64), 64), :] = jnp.dot(
            turn[...], acts[0], preferred_element_type=F32
        ).astype(BF16)
        return carry

    lax.fori_loop(0, ROWS // 64, turn_rows, 0)

    def send_more(j, carry):
        send_piece(j)
        return carry

    lax.fori_loop(2, ANSWERED, send_more, 0)

    block, place = table_rows()

    def fill(i, carry):
        t = i // 4
        p = i % 4
        for b in range(8):
            rows = []
            for n in range(8):
                l = p * 8 + n
                hit = (tables[t, b, 0, pl.ds(l, 1), :] == place) & (block == b)
                rows.append(jnp.where(hit, tables[t, b, 1, pl.ds(l, 1), :], 0.0))
            whole = jnp.concatenate(rows, axis=0)
            mix[t, b * TOK : (b + 1) * TOK, pl.ds(pl.multiple_of(p * 8 * MSG, TOK), 8 * MSG)] = whole.T.astype(BF16)
        return carry

    lax.fori_loop(0, TYPES * PLANE // 8, fill, 0)

    def reduce_piece(j):
        t = j % 3
        here = turned(t)
        for k, o in enumerate(OFFSETS):
            message(k, j, t, here, from_plane(o, here)).wait_recv()

        @pl.when(j >= 2)
        def _():
            sent_columns(j - 2)

        def tile(i, carry):
            rows = pl.ds(pl.multiple_of(i * 256, 256), 256)
            partial[j % 2, rows, :] = jnp.dot(mix[t, rows, :], got[j], preferred_element_type=F32).astype(BF16)
            return carry

        lax.fori_loop(0, 4, tile, 0)
        for n, o in enumerate(COLUMN):
            column_copy(n, j, t, to_column(o, here), here).start()
        me = here[2] * 2 + here[3]
        sums[j, here[2], here[3]] = partial[j % 2, pl.ds(pl.multiple_of(me * TOK, TOK), TOK), :]

    def finish_piece(j):
        t = j % 3
        here = turned(t)
        for n, o in enumerate(COLUMN):
            column_copy(n, j, t, here, from_column(o, here)).wait_recv()
        for half in range(2):
            span = pl.ds(pl.multiple_of(half * HALF + j * PIECE, PIECE), PIECE)
            total = hidden[:, span]
            for n in range(4):
                total = total + sums[j, n, half].astype(F32)
            out[:, span] = total.astype(BF16)

    def step(j, carry):
        @pl.when(j < PIECES)
        def _():
            reduce_piece(j)

        @pl.when(j < PIECES - ANSWERED)
        def _():
            sent(j)
            send_piece(j + ANSWERED)

        @pl.when(j >= 1)
        def _():
            finish_piece(j - 1)

        return carry

    lax.fori_loop(0, PIECES + 1, step, 0)

    for j in range(PIECES - ANSWERED, PIECES):
        sent(j)
    for j in range(PIECES - 2, PIECES):
        sent_columns(j)


def combine(act, tables, w_down, hidden):
    hbm = pl.BlockSpec(memory_space=pltpu.HBM)
    dma = pltpu.SemaphoreType.DMA
    return pl.pallas_call(
        combine_kernel,
        name="combine",
        out_shape=jax.ShapeDtypeStruct((TOK, D), BF16),
        in_specs=[hbm] * 4,
        out_specs=pl.BlockSpec(memory_space=pltpu.VMEM),
        scratch_shapes=[
            pltpu.VMEM((TYPES, ROWS, FF), BF16),
            pltpu.VMEM((TYPES, 8, 2, PLANE, TOK), F32),
            pltpu.VMEM((FF, D), BF16),
            pltpu.VMEM((TOK, D), F32),
            pltpu.VMEM((ANSWERED, 2, ROWS, PIECE), BF16),
            pltpu.VMEM((PIECES, ALL, PIECE), BF16),
            pltpu.VMEM((TYPES, 8 * TOK, ALL), BF16),
            pltpu.VMEM((2, 8 * TOK, PIECE), BF16),
            pltpu.VMEM((PIECES, 4, 2, TOK, PIECE), BF16),
            pltpu.VMEM((320, 320), BF16),
            pltpu.VMEM((64, ROWS), BF16),
            dma((4,)),
            dma((PIECES, len(OFFSETS))),
            dma((PIECES, len(OFFSETS))),
            dma((PIECES, len(COLUMN))),
            dma((PIECES, len(COLUMN))),
        ],
        compiler_params=pltpu.CompilerParams(
            collective_id=3, has_side_effects=True, vmem_limit_bytes=62 * 2**20
        ),
    )(act, tables, w_down, hidden)


def body(
    queries, fresh_keys, fresh_values, stored_keys, stored_values, column_blocks, diagonal_offsets,
    residual, norm_gain, routes, gate_weights, w_gate, w_up, w_down,
):
    kv = exchange(*collect(column_blocks, diagonal_offsets, stored_keys, stored_values))
    hidden, normed, table = attend(
        column_blocks, diagonal_offsets, queries, fresh_keys, fresh_values, kv,
        residual, norm_gain, routes, gate_weights,
    )
    act, tables = dispatch(normed, table, w_gate[0], w_up[0])
    return combine(act, tables, w_down[0], hidden)


def solution(mesh):
    rows = P(("ctx", "exp"), None)
    experts = P(("ctx", "exp"), None, None)
    in_specs = (
        rows, rows, rows, P("ctx", None), P("ctx", None), P(), P(), rows, P(), rows, rows,
        experts, experts, experts,
    )
    return jax.shard_map(body, mesh=mesh, in_specs=in_specs, out_specs=rows, check_vma=False)
```

```python
import functools

import jax
import jax.numpy as jnp
from jax import lax
from jax.experimental import pallas as pl
from jax.experimental.pallas import tpu as pltpu
from jax.sharding import PartitionSpec as P

MESH = pl.DeviceIdType.MESH
BF16 = jnp.bfloat16
F32 = jnp.float32
BLOCK = 64
HEAD = 128
HEADS_KV = 2
GROUP = 16
VERT = 2
SLASH = 8
SLOTS = VERT + 2 * SLASH
TOK = 128
D = 4096
FF = 768
HALF = D // 2
CAP = 10
PLANE = 32
MSG = 8 * CAP
ROWS = 16 * MSG
ALL = PLANE * MSG
PIECE = 256
PIECES = HALF // PIECE
NEG = -1e30


STAGED = 5
AHEAD = 4
BEHIND = 3
ANSWERED = 4
TYPES = 3


def coords():
    ctx = lax.axis_index("ctx")
    exp = lax.axis_index("exp")
    return ((exp // 4) % 2) * 2 + ctx // 2, exp % 4, exp // 8, ctx % 2


def device(x, y, z, c):
    return ((x % 2) * 2 + c, z * 8 + (x // 2) * 4 + y)


def unit(t):
    return (2 - t) * (1 - t) // 2, t * (2 - t), t * (t - 1) // 2


def turned(t):
    x, y, z, c = coords()
    t0, t1, t2 = unit(t)
    return x * (t0 + t1) + y * t2, y * t0 + z * (t1 + t2), z * t0 + y * t1 + x * t2, c


def turned_device(t, dev):
    p, q, a, c = dev
    t0, t1, t2 = unit(t)
    return device(p * (t0 + t1) + a * t2, q * t0 + a * t1 + p * t2, a * t0 + q * (t1 + t2), c)


def plane_index(dev):
    return (dev[0] * 4 + dev[1]) * 2 + dev[3]


def ordered_offsets():
    left = [(dx, dy, dc) for dx in range(4) for dy in range(4) for dc in range(2) if dx or dy or dc]
    use = {}
    out = []

    def links(o):
        found = []
        for axis in range(2):
            if o[axis] == 1:
                found.append((axis, 1))
            elif o[axis] == 3:
                found.append((axis, -1))
            elif o[axis] == 2:
                found += [(axis, 1), (axis, -1)]
        return found

    while left:
        best = min(left, key=lambda o: (sum(2 * use.get(k, 0) + 1 for k in links(o)), -len(links(o)), o))
        left.remove(best)
        out.append(best)
        for k in links(best):
            use[k] = use.get(k, 0) + 1
    return out


OFFSETS = ordered_offsets()
COLUMN = [(1, 0), (3, 1), (2, 0), (3, 0), (1, 1), (2, 1), (0, 1)]
PEERS = [
    (dx, dy, dz, dc)
    for dx in range(4)
    for dy in range(4)
    for dz in range(4)
    for dc in range(2)
    if dx * dy * dz == 0 and (dx or dy or dz or dc)
]


def to_plane(o, dev):
    return (dev[0] + o[0]) % 4, (dev[1] + o[1]) % 4, dev[2], (dev[3] + o[2]) % 2


def from_plane(o, dev):
    return (dev[0] + 4 - o[0]) % 4, (dev[1] + 4 - o[1]) % 4, dev[2], (dev[3] + 2 - o[2]) % 2


def to_column(o, dev):
    return dev[0], dev[1], (dev[2] + o[0]) % 4, (dev[3] + o[1]) % 2


def from_column(o, dev):
    return dev[0], dev[1], (dev[2] + 4 - o[0]) % 4, (dev[3] + 2 - o[1]) % 2


CUTS = (0, 11, 21, 31)


def roll(start, step):
    kinds = [(step + 3 - i) % 3 for i in range(3)]
    places = [turned(t) for t in kinds]
    steady = (step >= 2) & (step < PIECES)

    @pl.when(steady)
    def _():
        for n in range(CUTS[1]):
            for i in range(3):
                if CUTS[i] + n < CUTS[i + 1]:
                    start(CUTS[i] + n, step - i, kinds[i], places[i])

    for i in range(3):

        @pl.when(jnp.logical_not(steady) & (step >= i) & (step - i < PIECES))
        def _():
            for k in range(CUTS[i], CUTS[i + 1]):
                start(k, step - i, kinds[i], places[i])


def greet_all():
    bar = pltpu.get_barrier_semaphore()
    x, y, z, c = coords()
    for o in PEERS:
        other = device((x + o[0]) % 4, (y + o[1]) % 4, (z + o[2]) % 4, (c + o[3]) % 2)
        pl.semaphore_signal(bar, inc=1, device_id=other, device_id_type=MESH)
    pl.semaphore_wait(bar, len(PEERS))


def digits(row):
    n = (row * 3277) >> 16
    return n >> 4, (n >> 2) & 3, n & 3, row - n * 20


def swap_matrix():
    row = lax.broadcasted_iota(jnp.int32, (320, 1), 0)
    _, d2, d1, rest = digits(row)
    source = d1 * 80 + d2 * 20 + rest
    return (lax.broadcasted_iota(jnp.int32, (320, 320), 1) == source).astype(F32).astype(BF16)


def turn_matrix(rows, start, back):
    row = lax.broadcasted_iota(jnp.int32, (rows, 1), 0) + start
    d3, d2, d1, rest = digits(row)
    source = d1 * 320 + d3 * 80 + d2 * 20 + rest if back else d2 * 320 + d1 * 80 + d3 * 20 + rest
    return (lax.broadcasted_iota(jnp.int32, (rows, ROWS), 1) == source).astype(F32).astype(BF16)


def side(h):
    exp = lax.axis_index("exp")
    return exp + h * (4 - 8 * ((exp // 4) % 2))


def collect_kernel(cols, offs, keys_hbm, values_hbm, con, near, bias_out, keys, values, sem):
    loads = [pltpu.make_async_copy(keys_hbm, keys, sem.at[0]), pltpu.make_async_copy(values_hbm, values, sem.at[1])]
    for load in loads:
        load.start()
    ctx = lax.axis_index("ctx")
    xl = ctx // 2
    lane = lax.broadcasted_iota(jnp.int32, (8, (VERT + SLASH) * BLOCK), 1) // BLOCK
    for h in range(HEADS_KV):
        for i in range(2):
            block = 128 + 2 * (ctx * 32 + lax.axis_index("exp")) + i
            listed = [cols[h, v] for v in range(VERT)] + [block - offs[h, s] for s in range(SLASH)]
            bias = jnp.zeros(lane.shape, F32)
            for n, one in enumerate(listed):
                kept = (one >= 0) & (one < 128)
                for before in listed[:n]:
                    kept = kept & (one != before)
                bias = jnp.where(lane == n, jnp.where(kept, 0.0, NEG), bias)
            bias_out[h * 2 + i] = bias
    for load in loads:
        load.wait()

    def put(h, slot, block_a, block_b):
        near_a = block_a - 32 * ctx
        near_b = block_b - 32 * ctx
        local = jnp.where((near_a >= 0) & (near_a < 32), near_a, near_b)
        inside = (local >= 0) & (local < 32)
        start = pl.multiple_of(jnp.clip(local, 0, 31) * BLOCK, BLOCK)
        factor = jnp.where(inside, 1.0, 0.0).astype(BF16)
        for kind, ref in ((0, keys), (1, values)):
            block = ref[pl.ds(start, BLOCK), h * HEAD : (h + 1) * HEAD]
            con[kind, h, slot * BLOCK : (slot + 1) * BLOCK, :] = block * factor

    for h in range(HEADS_KV):
        exp = jnp.where(xl == 0, side(h), side(0))
        for v in range(VERT):
            put(h, v, cols[h, v], cols[h, v])
            here = (cols[h, v] // 64) == xl
            near[h * SLOTS + v] = jnp.full((8, HEAD), jnp.where(here, 1.0, 0.0), F32)
        for i in range(2):
            for s in range(SLASH):
                block_2 = 256 + 2 * exp + i - offs[h, s]
                slot = VERT + i * SLASH + s
                put(h, slot, block_2, block_2 + 64)
                near[h * SLOTS + slot] = jnp.full((8, HEAD), jnp.where(block_2 >= 0, 1.0, 0.0), F32)


def collect(cols, offs, keys, values):
    return pl.pallas_call(
        collect_kernel,
        name="collect_blocks",
        out_shape=[
            jax.ShapeDtypeStruct((2, HEADS_KV, SLOTS * BLOCK, HEAD), BF16),
            jax.ShapeDtypeStruct((HEADS_KV * SLOTS, 8, HEAD), F32),
            jax.ShapeDtypeStruct((HEADS_KV * 2, 8, (VERT + SLASH) * BLOCK), F32),
        ],
        in_specs=[pl.BlockSpec(memory_space=pltpu.SMEM)] * 2 + [pl.BlockSpec(memory_space=pltpu.HBM)] * 2,
        out_specs=[pl.BlockSpec(memory_space=pltpu.VMEM)] * 3,
        scratch_shapes=[
            pltpu.VMEM((2048, HEADS_KV * HEAD), BF16),
            pltpu.VMEM((2048, HEADS_KV * HEAD), BF16),
            pltpu.SemaphoreType.DMA((2,)),
        ],
        compiler_params=pltpu.CompilerParams(vmem_limit_bytes=60 * 2**20),
    )(cols, offs, keys, values)


def front_kernel(
    con_hbm, near_hbm, routes_hbm, gates_hbm, q_hbm, bias_hbm, fk_hbm, fv_hbm, res_hbm, gain_hbm,
    hidden_out, normed_out, table_out,
    con, near, routes, gates, q, bias_all, fk, fv, res, gain, hidden, normed, table,
    out, sib, chip, rem, fin, arr, in_sem, sem, ssem, rsem,
):
    given = (con_hbm, near_hbm, routes_hbm, gates_hbm, q_hbm, bias_hbm, fk_hbm, fv_hbm, res_hbm, gain_hbm)
    held = (con, near, routes, gates, q, bias_all, fk, fv, res, gain)
    loads = [pltpu.make_async_copy(src, dst, in_sem.at[n]) for n, (src, dst) in enumerate(zip(given, held))]
    for load in loads:
        load.start()
    puts = []

    def put(src, dst):
        copy = pltpu.make_async_copy(src, dst, sem.at[len(puts)])
        copy.start()
        puts.append(copy)

    x, y, z, c = coords()
    xl = x % 2
    exp = lax.axis_index("exp")
    twin = (xl * 2 + 1 - c, exp)
    across = [((1 - xl) * 2 + c, side(h)) for h in range(HEADS_KV)]
    bar = pltpu.get_barrier_semaphore()
    for other in (twin, *across):
        pl.semaphore_signal(bar, inc=1, device_id=other, device_id_type=MESH)
    pl.semaphore_wait(bar, 3)
    for load in loads[:2]:
        load.wait()

    first = pltpu.make_async_remote_copy(
        src_ref=con.at[1 - c], dst_ref=sib, send_sem=ssem.at[0], recv_sem=rsem.at[0],
        device_id=twin, device_id_type=MESH,
    )
    first.start()
    first.wait()
    chip[...] = con[c] + sib[...]

    verts = VERT * BLOCK

    def whole(h):
        return pltpu.make_async_remote_copy(
            src_ref=chip.at[h], dst_ref=rem.at[h], send_sem=ssem.at[1 + h], recv_sem=rsem.at[1 + h],
            device_id=across[h], device_id_type=MESH,
        )

    def vertical(h):
        return pltpu.make_async_remote_copy(
            src_ref=chip.at[h, pl.ds(0, verts)], dst_ref=rem.at[h, pl.ds(0, verts)],
            send_sem=ssem.at[1 + h], recv_sem=rsem.at[1 + h],
            device_id=across[h], device_id_type=MESH,
        )

    @pl.when(xl == 0)
    def _():
        for h in range(HEADS_KV):
            whole(h).start()

    @pl.when(xl == 1)
    def _():
        for h in range(HEADS_KV):
            vertical(h).start()

    for load in loads[2:]:
        load.wait()

    ids = routes[...]
    group, rest = ids >> 5, ids & 31
    ex, ey, ez, ec = ((rest >> 2) & 1) * 2 + (group >> 1), rest & 3, rest >> 3, group & 1
    lanes = lax.broadcasted_iota(jnp.int32, (TOK, TOK), 1)
    subs = lax.broadcasted_iota(jnp.int32, (TOK, TOK), 0)
    later = (subs < lanes).astype(F32).astype(BF16)
    for t, (p, r, a) in enumerate(((ex, ey, ez), (ex, ez, ey), (ey, ez, ex))):
        number = a * PLANE + (p * 4 + r) * 2 + ec
        named = jnp.zeros((TOK, TOK), F32)
        strength = jnp.zeros((TOK, TOK), F32)
        for n in range(8):
            hit = number[n : n + 1, :] == subs
            named = named + jnp.where(hit, 1.0, 0.0)
            strength = strength + jnp.where(hit, gates[n : n + 1, :], 0.0)
        place = jnp.dot(named.astype(BF16), later, preferred_element_type=F32)
        place = jnp.where(named > 0.5, place, -1.0).astype(BF16)
        strength = strength.astype(BF16)
        for n in range(4):
            table[t, n, 0] = place[n * PLANE : (n + 1) * PLANE]
            table[t, n, 1] = strength[n * PLANE : (n + 1) * PLANE]
    put(table, table_out)

    def back(h):
        return pltpu.make_async_remote_copy(
            src_ref=fin.at[h], dst_ref=arr.at[h], send_sem=ssem.at[3 + h], recv_sem=rsem.at[3 + h],
            device_id=twin, device_id_type=MESH,
        )

    def pick(h, slot):
        span = slice(slot * BLOCK, (slot + 1) * BLOCK)
        local = near[h * SLOTS + slot, 0:1, :].astype(BF16)
        far = rem[h, span, :]
        return span, chip[h, span, :] * local + far * (1.0 - local).astype(BF16), far

    def pick_verticals(h):
        for v in range(VERT):
            span, mixed, _ = pick(h, v)
            fin[h, span, :] = mixed
            out[c, h, span, :] = mixed

    for h in range(HEADS_KV):

        @pl.when(xl == 0)
        def _():
            vertical(h).wait_recv()
            pick_verticals(h)
            fin[h, verts:, :] = jnp.zeros((2 * SLASH * BLOCK, HEAD), BF16)
            out[c, h, verts:, :] = jnp.zeros((2 * SLASH * BLOCK, HEAD), BF16)

        @pl.when(xl == 1)
        def _():
            whole(h).wait_recv()
            pick_verticals(h)
            for slot in range(VERT, SLOTS):
                span, mixed, far = pick(h, slot)

                @pl.when(c == 1)
                def _():
                    out[1, h, span, :] = mixed
                    fin[h, span, :] = far

                @pl.when(c == 0)
                def _():
                    out[0, h, span, :] = far
                    fin[h, span, :] = mixed

        back(h).start()

    for h in range(HEADS_KV):
        back(h).wait()
        out[1 - c, h] = arr[h]

    @pl.when(xl == 0)
    def _():
        for h in range(HEADS_KV):
            whole(h).wait_send()

    @pl.when(xl == 1)
    def _():
        for h in range(HEADS_KV):
            vertical(h).wait_send()

    scale = 1.0 / HEAD**0.5
    heads = 4
    ones = jnp.ones(((VERT + SLASH) * BLOCK, HEAD), BF16)
    for h in range(HEADS_KV):
        for i in range(2):
            bias = bias_all[h * 2 + i, 0:1, :]
            slash = VERT * BLOCK + i * SLASH * BLOCK
            k = jnp.concatenate([out[0, h, : VERT * BLOCK, :], out[0, h, slash : slash + SLASH * BLOCK, :]], axis=0)
            v = jnp.concatenate([out[1, h, : VERT * BLOCK, :], out[1, h, slash : slash + SLASH * BLOCK, :]], axis=0)
            v = jnp.concatenate([v, ones], axis=1)
            rows = slice(i * BLOCK, (i + 1) * BLOCK)
            own_k = fk[rows, h * HEAD : (h + 1) * HEAD].astype(F32)
            own_v = fv[rows, h * HEAD : (h + 1) * HEAD].astype(F32)
            own_k = jnp.concatenate([own_k] * heads, axis=0)
            own_v = jnp.concatenate([own_v] * heads, axis=0)
            for g in range(0, GROUP, heads):
                spans = [slice((h * GROUP + g + n) * HEAD, (h * GROUP + g + n + 1) * HEAD) for n in range(heads)]
                part = jnp.concatenate([q[rows, span] for span in spans], axis=0)
                scores = lax.dot_general(part, k, (((1,), (1,)), ((), ())), preferred_element_type=F32)
                scores = scores * scale + bias
                own = jnp.sum(part.astype(F32) * own_k, axis=1, keepdims=True) * scale
                top = jnp.maximum(own, jnp.max(scores, axis=1, keepdims=True))
                weights = jnp.exp(scores - top).astype(BF16)
                own_weight = jnp.exp(own - top).astype(BF16).astype(F32)
                both = jnp.dot(weights, v, preferred_element_type=F32)
                numer = both[:, :HEAD] + own_weight * own_v
                denom = both[:, HEAD:] + own_weight
                attended = numer / denom
                for n, span in enumerate(spans):
                    hidden[rows, span] = res[rows, span].astype(F32) + attended[n * BLOCK : (n + 1) * BLOCK]
            done = hidden.at[pl.ds(i * BLOCK, BLOCK), pl.ds(h * GROUP * HEAD, GROUP * HEAD)]
            put(done, hidden_out.at[pl.ds(i * BLOCK, BLOCK), pl.ds(h * GROUP * HEAD, GROUP * HEAD)])

    for r in range(0, TOK, 16):
        part = hidden[r : r + 16, :]
        spread = jnp.mean(part * part, axis=1, keepdims=True)
        normed[r : r + 16, :] = (part * lax.rsqrt(spread + 1e-6) * gain[...]).astype(BF16)

    put(normed, normed_out)
    for copy in puts:
        copy.wait()


def front(con, near, bias, q, fk, fv, res, gain, routes, gates):
    part = (HEADS_KV, SLOTS * BLOCK, HEAD)
    hbm = pl.BlockSpec(memory_space=pltpu.HBM)
    args = (con, near, routes.T, gates.T, q, bias, fk, fv, res, gain.reshape(1, D))
    shapes = [((TOK, D), F32), ((TOK, D), BF16), ((TYPES, 4, 2, PLANE, TOK), BF16)]
    return pl.pallas_call(
        front_kernel,
        name="exchange_and_attention",
        out_shape=[jax.ShapeDtypeStruct(*one) for one in shapes],
        in_specs=[hbm] * len(args),
        out_specs=[hbm] * 3,
        scratch_shapes=[pltpu.VMEM(one.shape, one.dtype) for one in args]
        + [pltpu.VMEM(*one) for one in shapes]
        + [pltpu.VMEM((2,) + part, BF16)]
        + [pltpu.VMEM(part, BF16)] * 5
        + [
            pltpu.SemaphoreType.DMA((len(args),)),
            pltpu.SemaphoreType.DMA((6,)),
            pltpu.SemaphoreType.DMA((5,)),
            pltpu.SemaphoreType.DMA((5,)),
        ],
        compiler_params=pltpu.CompilerParams(
            collective_id=1, has_side_effects=True, vmem_limit_bytes=60 * 2**20
        ),
    )(*args)


def table_rows():
    row = lax.broadcasted_iota(jnp.int32, (MSG, TOK), 0)
    block = jnp.zeros((MSG, TOK), jnp.int32)
    for b in range(1, 8):
        block = block + jnp.where(row >= b * CAP, 1, 0)
    return block, (row - block * CAP).astype(F32)


def dispatch_kernel(
    normed_hbm, table_hbm, w_gate, w_up, act, tables_out,
    normed, table, x_all, tables, select, stage, got, weights, acc, swap, turn, sorted_rows,
    in_sem, w_sem, tab_s, tab_r, col_s, col_r, msg_s, msg_r,
):
    loads = [
        pltpu.make_async_copy(table_hbm, table, in_sem.at[0]),
        pltpu.make_async_copy(normed_hbm, normed, in_sem.at[1]),
    ]
    for load in loads:
        load.start()

    def weight_loads(j):
        return [
            pltpu.make_async_copy(
                w.at[pl.ds(pl.multiple_of(half * HALF + j * PIECE, PIECE), PIECE)],
                weights.at[j % 2, n, half],
                w_sem.at[j % 2, n, half],
            )
            for n, w in enumerate((w_gate, w_up))
            for half in range(2)
        ]

    for j in range(2):
        for load in weight_loads(j):
            load.start()
    greet_all()
    for load in loads:
        load.wait()

    def table_copy(n, t, dev, slot):
        return pltpu.make_async_remote_copy(
            src_ref=table.at[t, dev[2]], dst_ref=tables.at[t, slot], send_sem=tab_s.at[t, n], recv_sem=tab_r.at[t, n],
            device_id=turned_device(t, dev), device_id_type=MESH,
        )

    def column_copy(n, j, t, dev, slot):
        start = pl.multiple_of(dev[3] * HALF + j * PIECE, PIECE)
        return pltpu.make_async_remote_copy(
            src_ref=normed.at[:, pl.ds(start, PIECE)],
            dst_ref=x_all.at[j, pl.ds(pl.multiple_of(slot * TOK, TOK), TOK)],
            send_sem=col_s.at[j, n], recv_sem=col_r.at[j, n],
            device_id=turned_device(t, dev), device_id_type=MESH,
        )

    for t in range(TYPES):
        here = turned(t)
        me = here[2] * 2 + here[3]
        for n, o in enumerate(COLUMN):
            table_copy(n, t, to_column(o, here), me).start()
        tables[t, me] = table[t, here[2]]

    def send_columns(j, carry):
        t = j % 3
        here = turned(t)
        me = here[2] * 2 + here[3]
        for n, o in enumerate(COLUMN):
            column_copy(n, j, t, to_column(o, here), me).start()
        start = pl.multiple_of(here[3] * HALF + j * PIECE, PIECE)
        x_all[j, pl.ds(pl.multiple_of(me * TOK, TOK), TOK), :] = normed[:, pl.ds(start, PIECE)]
        return carry

    lax.fori_loop(0, PIECES, send_columns, 0)

    for t in range(TYPES):
        here = turned(t)
        for n, o in enumerate(COLUMN):
            dev = from_column(o, here)
            table_copy(n, t, dev, dev[2] * 2 + dev[3]).wait()
    tables_out[...] = tables[...].astype(F32)

    block, place = table_rows()

    def fill(t):
        def one(l, carry):
            for b in range(8):
                row = tables_out[t, b, 0, pl.ds(l, 1), :]
                hit = (row == place) & (block == b)
                select[t, pl.ds(pl.multiple_of(l * MSG, 16), MSG), b * TOK : (b + 1) * TOK] = jnp.where(
                    hit, 1.0, 0.0
                ).astype(BF16)
            return carry

        lax.fori_loop(0, PLANE, one, 0)

    fill(0)

    def message(k, j, t, dev, src_dev):
        chip = src_dev[0] * 4 + src_dev[1]
        return pltpu.make_async_remote_copy(
            src_ref=stage.at[j % STAGED, pl.ds(pl.multiple_of(plane_index(dev) * MSG, 16), MSG)],
            dst_ref=got.at[j, src_dev[3], pl.ds(pl.multiple_of(chip * MSG, 16), MSG)],
            send_sem=msg_s.at[j, k], recv_sem=msg_r.at[j, k],
            device_id=turned_device(t, dev), device_id_type=MESH,
        )

    def sent(j):
        here = turned(j % 3)
        for k, o in enumerate(OFFSETS):
            message(k, j, j % 3, to_plane(o, here), here).wait_send()

    def send_piece(j):
        t = j % 3
        here = turned(t)
        for n, o in enumerate(COLUMN):
            dev = from_column(o, here)
            column_copy(n, j, t, dev, dev[2] * 2 + dev[3]).wait_recv()

        @pl.when(j >= STAGED)
        def _():
            sent(j - STAGED)

        step = ALL // 8

        def tile(i, carry):
            rows = pl.ds(pl.multiple_of(i * step, 16), step)
            stage[j % STAGED, rows, :] = jnp.dot(select[t, rows, :], x_all[j], preferred_element_type=F32).astype(BF16)
            return carry

        lax.fori_loop(0, 8, tile, 0)
        own_rows = pl.ds(pl.multiple_of(plane_index(here) * MSG, 16), MSG)
        own_place = pl.ds(pl.multiple_of((here[0] * 4 + here[1]) * MSG, 16), MSG)
        got[j, here[3], own_place, :] = stage[j % STAGED, own_rows, :]

    def start(k, j, t, here):
        message(k, j, t, to_plane(OFFSETS[k], here), here).start()

    def use_piece(j):
        t = j % 3
        here = turned(t)
        for load in weight_loads(j):
            load.wait()
        for k, o in enumerate(OFFSETS):
            message(k, j, t, here, from_plane(o, here)).wait_recv()

        @pl.when(t == 0)
        def _():
            sorted_rows[...] = got[j]

        @pl.when(t == 1)
        def _():
            for half in range(2):
                for i in range(4):
                    rows = slice(i * 320, (i + 1) * 320)
                    sorted_rows[half, rows, :] = jnp.dot(
                        swap[...], got[j, half, rows, :], preferred_element_type=F32
                    ).astype(BF16)

        @pl.when(t == 2)
        def _():
            def tile(i, carry):
                rows = pl.ds(pl.multiple_of(i * 320, 16), 320)
                turn[...] = turn_matrix(320, i * 320, False)
                for half in range(2):
                    sorted_rows[half, rows, :] = jnp.dot(
                        turn[...], got[j, half], preferred_element_type=F32
                    ).astype(BF16)
                return carry

            lax.fori_loop(0, 4, tile, 0)

        step = ROWS // 5

        def tile(i, carry):
            rows = pl.ds(pl.multiple_of(i * step, 16), step)
            left = sorted_rows[0, rows, :]
            right = sorted_rows[1, rows, :]
            for n in range(2):
                acc[n, rows, :] += jnp.dot(left, weights[j % 2, n, 0], preferred_element_type=F32) + jnp.dot(
                    right, weights[j % 2, n, 1], preferred_element_type=F32
                )
            return carry

        lax.fori_loop(0, 5, tile, 0)

        @pl.when(j + 2 < PIECES)
        def _():
            for load in weight_loads(j + 2):
                load.start()

    def step(j, carry):
        @pl.when(j < PIECES)
        def _():
            send_piece(j)

        roll(start, j)

        @pl.when(j == 0)
        def _():
            acc[...] = jnp.zeros_like(acc)
            swap[...] = swap_matrix()

        @pl.when(j < 2)
        def _():
            fill(j + 1)

        @pl.when(j >= AHEAD)
        def _():
            use_piece(j - AHEAD)

        return carry

    lax.fori_loop(0, PIECES + AHEAD, step, 0)

    def finish(i, carry):
        rows = pl.ds(pl.multiple_of(i * MSG, 16), MSG)
        g = acc[0, rows, :]
        act[rows, :] = (g / (1.0 + jnp.exp(-g)) * acc[1, rows, :]).astype(BF16)
        return carry

    lax.fori_loop(0, ROWS // MSG, finish, 0)

    for j in range(PIECES - STAGED, PIECES):
        sent(j)

    def sent_columns(j, carry):
        here = turned(j % 3)
        for n, o in enumerate(COLUMN):
            column_copy(n, j, j % 3, to_column(o, here), here[2] * 2 + here[3]).wait_send()
        return carry

    lax.fori_loop(0, PIECES, sent_columns, 0)


def dispatch(normed, table, w_gate, w_up):
    vmem = pl.BlockSpec(memory_space=pltpu.VMEM)
    hbm = pl.BlockSpec(memory_space=pltpu.HBM)
    dma = pltpu.SemaphoreType.DMA
    return pl.pallas_call(
        dispatch_kernel,
        name="dispatch",
        out_shape=[
            jax.ShapeDtypeStruct((ROWS, FF), BF16),
            jax.ShapeDtypeStruct((TYPES, 8, 2, PLANE, TOK), F32),
        ],
        in_specs=[hbm] * 4,
        out_specs=[vmem] * 2,
        scratch_shapes=[
            pltpu.VMEM((TOK, D), BF16),
            pltpu.VMEM((TYPES, 4, 2, PLANE, TOK), BF16),
            pltpu.VMEM((PIECES, 8 * TOK, PIECE), BF16),
            pltpu.VMEM((TYPES, 8, 2, PLANE, TOK), BF16),
            pltpu.VMEM((TYPES, ALL, 8 * TOK), BF16),
            pltpu.VMEM((STAGED, ALL, PIECE), BF16),
            pltpu.VMEM((PIECES, 2, ROWS, PIECE), BF16),
            pltpu.VMEM((2, 2, 2, PIECE, FF), BF16),
            pltpu.VMEM((2, ROWS, FF), F32),
            pltpu.VMEM((320, 320), BF16),
            pltpu.VMEM((320, ROWS), BF16),
            pltpu.VMEM((2, ROWS, PIECE), BF16),
            dma((2,)),
            dma((2, 2, 2)),
            dma((TYPES, len(COLUMN))),
            dma((TYPES, len(COLUMN))),
            dma((PIECES, len(COLUMN))),
            dma((PIECES, len(COLUMN))),
            dma((PIECES, len(OFFSETS))),
            dma((PIECES, len(OFFSETS))),
        ],
        compiler_params=pltpu.CompilerParams(
            collective_id=2, has_side_effects=True, vmem_limit_bytes=62 * 2**20
        ),
    )(normed, table, w_gate, w_up)


def combine_kernel(
    act_hbm, tables_hbm, w_down, hidden_hbm, out,
    acts, tables, wd, hidden, answers, got, mix, partial, sums, swap, turn,
    in_sem, msg_s, msg_r, col_s, col_r,
):
    loads = [
        pltpu.make_async_copy(act_hbm, acts.at[0], in_sem.at[0]),
        pltpu.make_async_copy(w_down, wd, in_sem.at[1]),
        pltpu.make_async_copy(tables_hbm, tables, in_sem.at[2]),
        pltpu.make_async_copy(hidden_hbm, hidden, in_sem.at[3]),
    ]
    for load in loads:
        load.start()
    greet_all()
    for load in loads[:2]:
        load.wait()

    def message(k, j, t, dev, src_dev):
        chip = dev[0] * 4 + dev[1]
        return pltpu.make_async_remote_copy(
            src_ref=answers.at[j % ANSWERED, dev[3], pl.ds(pl.multiple_of(chip * MSG, 16), MSG)],
            dst_ref=got.at[j, pl.ds(pl.multiple_of(plane_index(src_dev) * MSG, 16), MSG)],
            send_sem=msg_s.at[j, k], recv_sem=msg_r.at[j, k],
            device_id=turned_device(t, dev), device_id_type=MESH,
        )

    def column_copy(n, j, t, dev, src_dev):
        block = dev[2] * 2 + dev[3]
        return pltpu.make_async_remote_copy(
            src_ref=partial.at[j, pl.ds(pl.multiple_of(block * TOK, TOK), TOK)],
            dst_ref=sums.at[j, src_dev[2], src_dev[3]],
            send_sem=col_s.at[j, n], recv_sem=col_r.at[j, n],
            device_id=turned_device(t, dev), device_id_type=MESH,
        )

    def sent(j):
        here = turned(j % 3)
        for k, o in enumerate(OFFSETS):
            message(k, j, j % 3, to_plane(o, here), here).wait_send()

    def sent_columns(j):
        here = turned(j % 3)
        for n, o in enumerate(COLUMN):
            column_copy(n, j, j % 3, to_column(o, here), here).wait_send()

    def send_piece(j):
        t = j % 3
        here = turned(t)
        for half in range(2):
            span = pl.ds(pl.multiple_of(half * HALF + j * PIECE, PIECE), PIECE)

            def tile(i, inner):
                rows = pl.ds(pl.multiple_of(i * (ROWS // 4), 16), ROWS // 4)
                answers[j % ANSWERED, half, rows, :] = jnp.dot(
                    acts[t, rows, :], wd[:, span], preferred_element_type=F32
                ).astype(BF16)
                return inner

            lax.fori_loop(0, 4, tile, 0)
        own_rows = pl.ds(pl.multiple_of(plane_index(here) * MSG, 16), MSG)
        own_place = pl.ds(pl.multiple_of((here[0] * 4 + here[1]) * MSG, 16), MSG)
        got[j, own_rows, :] = answers[j % ANSWERED, here[3], own_place, :]
        for k, o in enumerate(OFFSETS):
            message(k, j, t, to_plane(o, here), here).start()

    send_piece(0)
    swap[...] = swap_matrix()
    for i in range(4):
        rows = slice(i * 320, (i + 1) * 320)
        acts[1, rows, :] = jnp.dot(swap[...], acts[0, rows, :], preferred_element_type=F32).astype(BF16)
    send_piece(1)

    def turn_rows(i, carry):
        turn[...] = turn_matrix(64, i * 64, True)
        acts[2, pl.ds(pl.multiple_of(i * 64, 64), 64), :] = jnp.dot(
            turn[...], acts[0], preferred_element_type=F32
        ).astype(BF16)
        return carry

    lax.fori_loop(0, ROWS // 64, turn_rows, 0)

    def send_more(j, carry):
        send_piece(j)
        return carry

    lax.fori_loop(2, ANSWERED, send_more, 0)

    for load in loads[2:]:
        load.wait()
    block, place = table_rows()

    def fill(i, carry):
        t = i // 4
        p = i % 4
        for b in range(8):
            rows = []
            for n in range(8):
                l = p * 8 + n
                hit = (tables[t, b, 0, pl.ds(l, 1), :] == place) & (block == b)
                rows.append(jnp.where(hit, tables[t, b, 1, pl.ds(l, 1), :], 0.0))
            whole = jnp.concatenate(rows, axis=0)
            mix[t, b * TOK : (b + 1) * TOK, pl.ds(pl.multiple_of(p * 8 * MSG, TOK), 8 * MSG)] = whole.T.astype(BF16)
        return carry

    lax.fori_loop(0, TYPES * PLANE // 8, fill, 0)

    def reduce_piece(j):
        t = j % 3
        here = turned(t)
        for k, o in enumerate(OFFSETS):
            message(k, j, t, here, from_plane(o, here)).wait_recv()

        for far in (2, 1, 3, 0):
            rows = pl.ds(pl.multiple_of(((here[2] + far) % 4) * 2 * TOK, 2 * TOK), 2 * TOK)
            partial[j, rows, :] = jnp.dot(mix[t, rows, :], got[j], preferred_element_type=F32).astype(BF16)
            for n, o in enumerate(COLUMN):
                if o[0] == far:
                    column_copy(n, j, t, to_column(o, here), here).start()
        me = here[2] * 2 + here[3]
        sums[j, here[2], here[3]] = partial[j, pl.ds(pl.multiple_of(me * TOK, TOK), TOK), :]

    def finish_piece(j):
        t = j % 3
        here = turned(t)
        for n, o in enumerate(COLUMN):
            column_copy(n, j, t, here, from_column(o, here)).wait_recv()
        for half in range(2):
            span = pl.ds(pl.multiple_of(half * HALF + j * PIECE, PIECE), PIECE)
            total = hidden[:, span]
            for n in range(4):
                total = total + sums[j, n, half].astype(F32)
            out[:, span] = total.astype(BF16)

    def step(j, carry):
        @pl.when(j < PIECES)
        def _():
            reduce_piece(j)

        @pl.when(j < PIECES - ANSWERED)
        def _():
            sent(j)
            send_piece(j + ANSWERED)

        @pl.when(j >= BEHIND)
        def _():
            finish_piece(j - BEHIND)

        return carry

    lax.fori_loop(0, PIECES + BEHIND, step, 0)

    for j in range(PIECES - ANSWERED, PIECES):
        sent(j)
    for j in range(PIECES):
        sent_columns(j)


def combine(act, tables, w_down, hidden):
    hbm = pl.BlockSpec(memory_space=pltpu.HBM)
    dma = pltpu.SemaphoreType.DMA
    return pl.pallas_call(
        combine_kernel,
        name="combine",
        out_shape=jax.ShapeDtypeStruct((TOK, D), BF16),
        in_specs=[hbm] * 4,
        out_specs=pl.BlockSpec(memory_space=pltpu.VMEM),
        scratch_shapes=[
            pltpu.VMEM((TYPES, ROWS, FF), BF16),
            pltpu.VMEM((TYPES, 8, 2, PLANE, TOK), F32),
            pltpu.VMEM((FF, D), BF16),
            pltpu.VMEM((TOK, D), F32),
            pltpu.VMEM((ANSWERED, 2, ROWS, PIECE), BF16),
            pltpu.VMEM((PIECES, ALL, PIECE), BF16),
            pltpu.VMEM((TYPES, 8 * TOK, ALL), BF16),
            pltpu.VMEM((PIECES, 8 * TOK, PIECE), BF16),
            pltpu.VMEM((PIECES, 4, 2, TOK, PIECE), BF16),
            pltpu.VMEM((320, 320), BF16),
            pltpu.VMEM((64, ROWS), BF16),
            dma((4,)),
            dma((PIECES, len(OFFSETS))),
            dma((PIECES, len(OFFSETS))),
            dma((PIECES, len(COLUMN))),
            dma((PIECES, len(COLUMN))),
        ],
        compiler_params=pltpu.CompilerParams(
            collective_id=3, has_side_effects=True, vmem_limit_bytes=62 * 2**20
        ),
    )(act, tables, w_down, hidden)


def body(
    queries, fresh_keys, fresh_values, stored_keys, stored_values, column_blocks, diagonal_offsets,
    residual, norm_gain, routes, gate_weights, w_gate, w_up, w_down,
):
    con, near, bias = collect(column_blocks, diagonal_offsets, stored_keys, stored_values)
    hidden, normed, table = front(
        con, near, bias, queries, fresh_keys, fresh_values, residual, norm_gain, routes, gate_weights
    )
    act, tables = dispatch(normed, table, w_gate[0], w_up[0])
    return combine(act, tables, w_down[0], hidden)


def solution(mesh):
    rows = P(("ctx", "exp"), None)
    experts = P(("ctx", "exp"), None, None)
    in_specs = (
        rows, rows, rows, P("ctx", None), P("ctx", None), P(), P(), rows, P(), rows, rows,
        experts, experts, experts,
    )
    return jax.shard_map(body, mesh=mesh, in_specs=in_specs, out_specs=rows, check_vma=False)
```

```python
import functools

import jax
import jax.numpy as jnp
from jax import lax
from jax.experimental import pallas as pl
from jax.experimental.pallas import tpu as pltpu
from jax.sharding import PartitionSpec as P

MESH = pl.DeviceIdType.MESH
BF16 = jnp.bfloat16
F32 = jnp.float32
BLOCK = 64
HEAD = 128
HEADS_KV = 2
GROUP = 16
VERT = 2
SLASH = 8
SLOTS = VERT + 2 * SLASH
TOK = 128
D = 4096
FF = 768
HALF = D // 2
CAP = 10
PLANE = 32
MSG = 8 * CAP
ROWS = 16 * MSG
ALL = PLANE * MSG
PIECE = 256
PIECES = HALF // PIECE
NEG = -1e30


STAGED = 5
AHEAD = 4
BEHIND = 3
ANSWERED = 4
TYPES = 3


def coords():
    ctx = lax.axis_index("ctx")
    exp = lax.axis_index("exp")
    return ((exp // 4) % 2) * 2 + ctx // 2, exp % 4, exp // 8, ctx % 2


def device(x, y, z, c):
    return ((x % 2) * 2 + c, z * 8 + (x // 2) * 4 + y)


def unit(t):
    return (2 - t) * (1 - t) // 2, t * (2 - t), t * (t - 1) // 2


def turned(t):
    x, y, z, c = coords()
    t0, t1, t2 = unit(t)
    return x * (t0 + t1) + y * t2, y * t0 + z * (t1 + t2), z * t0 + y * t1 + x * t2, c


def turned_device(t, dev):
    p, q, a, c = dev
    t0, t1, t2 = unit(t)
    return device(p * (t0 + t1) + a * t2, q * t0 + a * t1 + p * t2, a * t0 + q * (t1 + t2), c)


def plane_index(dev):
    return (dev[0] * 4 + dev[1]) * 2 + dev[3]


def ordered_offsets():
    left = [(dx, dy, dc) for dx in range(4) for dy in range(4) for dc in range(2) if dx or dy or dc]
    use = {}
    out = []

    def links(o):
        found = []
        for axis in range(2):
            if o[axis] == 1:
                found.append((axis, 1))
            elif o[axis] == 3:
                found.append((axis, -1))
            elif o[axis] == 2:
                found += [(axis, 1), (axis, -1)]
        return found

    while left:
        best = min(left, key=lambda o: (sum(2 * use.get(k, 0) + 1 for k in links(o)), -len(links(o)), o))
        left.remove(best)
        out.append(best)
        for k in links(best):
            use[k] = use.get(k, 0) + 1
    return out


OFFSETS = ordered_offsets()
COLUMN = [(1, 0), (3, 1), (2, 0), (3, 0), (1, 1), (2, 1), (0, 1)]
PEERS = [
    (dx, dy, dz, dc)
    for dx in range(4)
    for dy in range(4)
    for dz in range(4)
    for dc in range(2)
    if dx * dy * dz == 0 and (dx or dy or dz or dc)
]


def to_plane(o, dev):
    return (dev[0] + o[0]) % 4, (dev[1] + o[1]) % 4, dev[2], (dev[3] + o[2]) % 2


def from_plane(o, dev):
    return (dev[0] + 4 - o[0]) % 4, (dev[1] + 4 - o[1]) % 4, dev[2], (dev[3] + 2 - o[2]) % 2


def to_column(o, dev):
    return dev[0], dev[1], (dev[2] + o[0]) % 4, (dev[3] + o[1]) % 2


def from_column(o, dev):
    return dev[0], dev[1], (dev[2] + 4 - o[0]) % 4, (dev[3] + 2 - o[1]) % 2


CUTS = (0, 11, 21, 31)


def roll(start, step):
    kinds = [(step + 3 - i) % 3 for i in range(3)]
    places = [turned(t) for t in kinds]
    steady = (step >= 2) & (step < PIECES)

    @pl.when(steady)
    def _():
        for n in range(CUTS[1]):
            for i in range(3):
                if CUTS[i] + n < CUTS[i + 1]:
                    start(CUTS[i] + n, step - i, kinds[i], places[i])

    for i in range(3):

        @pl.when(jnp.logical_not(steady) & (step >= i) & (step - i < PIECES))
        def _():
            for k in range(CUTS[i], CUTS[i + 1]):
                start(k, step - i, kinds[i], places[i])


def greet_all():
    bar = pltpu.get_barrier_semaphore()
    x, y, z, c = coords()
    for o in PEERS:
        other = device((x + o[0]) % 4, (y + o[1]) % 4, (z + o[2]) % 4, (c + o[3]) % 2)
        pl.semaphore_signal(bar, inc=1, device_id=other, device_id_type=MESH)
    pl.semaphore_wait(bar, len(PEERS))


def digits(row):
    n = (row * 3277) >> 16
    return n >> 4, (n >> 2) & 3, n & 3, row - n * 20


def swap_matrix():
    row = lax.broadcasted_iota(jnp.int32, (320, 1), 0)
    _, d2, d1, rest = digits(row)
    source = d1 * 80 + d2 * 20 + rest
    return (lax.broadcasted_iota(jnp.int32, (320, 320), 1) == source).astype(F32).astype(BF16)


def turn_matrix(rows, start, back):
    row = lax.broadcasted_iota(jnp.int32, (rows, 1), 0) + start
    d3, d2, d1, rest = digits(row)
    source = d1 * 320 + d3 * 80 + d2 * 20 + rest if back else d2 * 320 + d1 * 80 + d3 * 20 + rest
    return (lax.broadcasted_iota(jnp.int32, (rows, ROWS), 1) == source).astype(F32).astype(BF16)


def side(h):
    exp = lax.axis_index("exp")
    return exp + h * (4 - 8 * ((exp // 4) % 2))


def collect_kernel(cols, offs, keys_hbm, values_hbm, con, near, bias_out, keys, values, sem):
    loads = [pltpu.make_async_copy(keys_hbm, keys, sem.at[0]), pltpu.make_async_copy(values_hbm, values, sem.at[1])]
    for load in loads:
        load.start()
    ctx = lax.axis_index("ctx")
    xl = ctx // 2
    lane = lax.broadcasted_iota(jnp.int32, (8, (VERT + SLASH) * BLOCK), 1) // BLOCK
    for h in range(HEADS_KV):
        for i in range(2):
            block = 128 + 2 * (ctx * 32 + lax.axis_index("exp")) + i
            listed = [cols[h, v] for v in range(VERT)] + [block - offs[h, s] for s in range(SLASH)]
            bias = jnp.zeros(lane.shape, F32)
            for n, one in enumerate(listed):
                kept = (one >= 0) & (one < 128)
                for before in listed[:n]:
                    kept = kept & (one != before)
                bias = jnp.where(lane == n, jnp.where(kept, 0.0, NEG), bias)
            bias_out[h * 2 + i] = bias
    for load in loads:
        load.wait()

    def put(h, slot, block_a, block_b):
        near_a = block_a - 32 * ctx
        near_b = block_b - 32 * ctx
        local = jnp.where((near_a >= 0) & (near_a < 32), near_a, near_b)
        inside = (local >= 0) & (local < 32)
        start = pl.multiple_of(jnp.clip(local, 0, 31) * BLOCK, BLOCK)
        factor = jnp.where(inside, 1.0, 0.0).astype(BF16)
        for kind, ref in ((0, keys), (1, values)):
            block = ref[pl.ds(start, BLOCK), h * HEAD : (h + 1) * HEAD]
            con[kind, h, slot * BLOCK : (slot + 1) * BLOCK, :] = block * factor

    for h in range(HEADS_KV):
        exp = jnp.where(xl == 0, side(h), side(0))
        for v in range(VERT):
            put(h, v, cols[h, v], cols[h, v])
            here = (cols[h, v] // 64) == xl
            near[h * SLOTS + v] = jnp.full((8, HEAD), jnp.where(here, 1.0, 0.0), F32)
        for i in range(2):
            for s in range(SLASH):
                block_2 = 256 + 2 * exp + i - offs[h, s]
                slot = VERT + i * SLASH + s
                put(h, slot, block_2, block_2 + 64)
                near[h * SLOTS + slot] = jnp.full((8, HEAD), jnp.where(block_2 >= 0, 1.0, 0.0), F32)


def collect(cols, offs, keys, values):
    return pl.pallas_call(
        collect_kernel,
        name="collect_blocks",
        out_shape=[
            jax.ShapeDtypeStruct((2, HEADS_KV, SLOTS * BLOCK, HEAD), BF16),
            jax.ShapeDtypeStruct((HEADS_KV * SLOTS, 8, HEAD), F32),
            jax.ShapeDtypeStruct((HEADS_KV * 2, 8, (VERT + SLASH) * BLOCK), F32),
        ],
        in_specs=[pl.BlockSpec(memory_space=pltpu.SMEM)] * 2 + [pl.BlockSpec(memory_space=pltpu.HBM)] * 2,
        out_specs=[pl.BlockSpec(memory_space=pltpu.VMEM)] * 3,
        scratch_shapes=[
            pltpu.VMEM((2048, HEADS_KV * HEAD), BF16),
            pltpu.VMEM((2048, HEADS_KV * HEAD), BF16),
            pltpu.SemaphoreType.DMA((2,)),
        ],
        compiler_params=pltpu.CompilerParams(vmem_limit_bytes=60 * 2**20),
    )(cols, offs, keys, values)


def front_kernel(
    con_hbm, near_hbm, routes_hbm, gates_hbm, q_hbm, bias_hbm, fk_hbm, fv_hbm, res_hbm, gain_hbm,
    hidden_out, normed_out, table_out,
    con, near, routes, gates, q, bias_all, fk, fv, res, gain, hidden, normed, table,
    out, sib, chip, rem, fin, arr, in_sem, sem, ssem, rsem,
):
    given = (con_hbm, near_hbm, routes_hbm, gates_hbm, q_hbm, bias_hbm, fk_hbm, fv_hbm, res_hbm, gain_hbm)
    held = (con, near, routes, gates, q, bias_all, fk, fv, res, gain)
    loads = [pltpu.make_async_copy(src, dst, in_sem.at[n]) for n, (src, dst) in enumerate(zip(given, held))]
    for load in loads:
        load.start()
    puts = []

    def put(src, dst):
        copy = pltpu.make_async_copy(src, dst, sem.at[len(puts)])
        copy.start()
        puts.append(copy)

    x, y, z, c = coords()
    xl = x % 2
    exp = lax.axis_index("exp")
    twin = (xl * 2 + 1 - c, exp)
    across = [((1 - xl) * 2 + c, side(h)) for h in range(HEADS_KV)]
    bar = pltpu.get_barrier_semaphore()
    for other in (twin, *across):
        pl.semaphore_signal(bar, inc=1, device_id=other, device_id_type=MESH)
    pl.semaphore_wait(bar, 3)
    for load in loads[:2]:
        load.wait()

    verts = VERT * BLOCK

    def whole(h):
        return pltpu.make_async_remote_copy(
            src_ref=chip.at[h], dst_ref=rem.at[h], send_sem=ssem.at[1 + h], recv_sem=rsem.at[1 + h],
            device_id=across[h], device_id_type=MESH,
        )

    def vertical(h):
        return pltpu.make_async_remote_copy(
            src_ref=chip.at[h, pl.ds(0, verts)], dst_ref=rem.at[h, pl.ds(0, verts)],
            send_sem=ssem.at[1 + h], recv_sem=rsem.at[1 + h],
            device_id=across[h], device_id_type=MESH,
        )

    firsts = [
        pltpu.make_async_remote_copy(
            src_ref=con.at[1 - c, h], dst_ref=sib.at[h], send_sem=ssem.at[5 * h], recv_sem=rsem.at[5 * h],
            device_id=twin, device_id_type=MESH,
        )
        for h in range(HEADS_KV)
    ]
    for first in firsts:
        first.start()
    for h in range(HEADS_KV):
        firsts[h].wait()
        chip[h] = con[c, h] + sib[h]

        @pl.when(xl == 0)
        def _():
            whole(h).start()

        @pl.when(xl == 1)
        def _():
            vertical(h).start()

    for load in loads[2:]:
        load.wait()

    ids = routes[...]
    group, rest = ids >> 5, ids & 31
    ex, ey, ez, ec = ((rest >> 2) & 1) * 2 + (group >> 1), rest & 3, rest >> 3, group & 1
    lanes = lax.broadcasted_iota(jnp.int32, (TOK, TOK), 1)
    subs = lax.broadcasted_iota(jnp.int32, (TOK, TOK), 0)
    later = (subs < lanes).astype(F32).astype(BF16)
    for t, (p, r, a) in enumerate(((ex, ey, ez), (ex, ez, ey), (ey, ez, ex))):
        number = a * PLANE + (p * 4 + r) * 2 + ec
        named = jnp.zeros((TOK, TOK), F32)
        strength = jnp.zeros((TOK, TOK), F32)
        for n in range(8):
            hit = number[n : n + 1, :] == subs
            named = named + jnp.where(hit, 1.0, 0.0)
            strength = strength + jnp.where(hit, gates[n : n + 1, :], 0.0)
        place = jnp.dot(named.astype(BF16), later, preferred_element_type=F32)
        place = jnp.where(named > 0.5, place, -1.0).astype(BF16)
        strength = strength.astype(BF16)
        for n in range(4):
            table[t, n, 0] = place[n * PLANE : (n + 1) * PLANE]
            table[t, n, 1] = strength[n * PLANE : (n + 1) * PLANE]
    put(table, table_out)

    def back(h):
        return pltpu.make_async_remote_copy(
            src_ref=fin.at[h], dst_ref=arr.at[h], send_sem=ssem.at[3 + h], recv_sem=rsem.at[3 + h],
            device_id=twin, device_id_type=MESH,
        )

    def pick(h, slot):
        span = slice(slot * BLOCK, (slot + 1) * BLOCK)
        local = near[h * SLOTS + slot, 0:1, :].astype(BF16)
        far = rem[h, span, :]
        return span, chip[h, span, :] * local + far * (1.0 - local).astype(BF16), far

    def pick_verticals(h):
        for v in range(VERT):
            span, mixed, _ = pick(h, v)
            fin[h, span, :] = mixed
            out[c, h, span, :] = mixed

    for h in range(HEADS_KV):

        @pl.when(xl == 0)
        def _():
            vertical(h).wait_recv()
            pick_verticals(h)
            fin[h, verts:, :] = jnp.zeros((2 * SLASH * BLOCK, HEAD), BF16)
            out[c, h, verts:, :] = jnp.zeros((2 * SLASH * BLOCK, HEAD), BF16)

        @pl.when(xl == 1)
        def _():
            whole(h).wait_recv()
            pick_verticals(h)
            for slot in range(VERT, SLOTS):
                span, mixed, far = pick(h, slot)

                @pl.when(c == 1)
                def _():
                    out[1, h, span, :] = mixed
                    fin[h, span, :] = far

                @pl.when(c == 0)
                def _():
                    out[0, h, span, :] = far
                    fin[h, span, :] = mixed

        back(h).start()

    for h in range(HEADS_KV):
        back(h).wait()
        out[1 - c, h] = arr[h]

    @pl.when(xl == 0)
    def _():
        for h in range(HEADS_KV):
            whole(h).wait_send()

    @pl.when(xl == 1)
    def _():
        for h in range(HEADS_KV):
            vertical(h).wait_send()

    scale = 1.0 / HEAD**0.5
    heads = 4
    ones = jnp.ones(((VERT + SLASH) * BLOCK, HEAD), BF16)
    for h in range(HEADS_KV):
        for i in range(2):
            bias = bias_all[h * 2 + i, 0:1, :]
            slash = VERT * BLOCK + i * SLASH * BLOCK
            k = jnp.concatenate([out[0, h, : VERT * BLOCK, :], out[0, h, slash : slash + SLASH * BLOCK, :]], axis=0)
            v = jnp.concatenate([out[1, h, : VERT * BLOCK, :], out[1, h, slash : slash + SLASH * BLOCK, :]], axis=0)
            v = jnp.concatenate([v, ones], axis=1)
            rows = slice(i * BLOCK, (i + 1) * BLOCK)
            own_k = fk[rows, h * HEAD : (h + 1) * HEAD].astype(F32)
            own_v = fv[rows, h * HEAD : (h + 1) * HEAD].astype(F32)
            own_k = jnp.concatenate([own_k] * heads, axis=0)
            own_v = jnp.concatenate([own_v] * heads, axis=0)
            for g in range(0, GROUP, heads):
                spans = [slice((h * GROUP + g + n) * HEAD, (h * GROUP + g + n + 1) * HEAD) for n in range(heads)]
                part = jnp.concatenate([q[rows, span] for span in spans], axis=0)
                scores = lax.dot_general(part, k, (((1,), (1,)), ((), ())), preferred_element_type=F32)
                scores = scores * scale + bias
                own = jnp.sum(part.astype(F32) * own_k, axis=1, keepdims=True) * scale
                top = jnp.maximum(own, jnp.max(scores, axis=1, keepdims=True))
                weights = jnp.exp(scores - top).astype(BF16)
                own_weight = jnp.exp(own - top).astype(BF16).astype(F32)
                both = jnp.dot(weights, v, preferred_element_type=F32)
                numer = both[:, :HEAD] + own_weight * own_v
                denom = both[:, HEAD:] + own_weight
                attended = numer / denom
                for n, span in enumerate(spans):
                    hidden[rows, span] = res[rows, span].astype(F32) + attended[n * BLOCK : (n + 1) * BLOCK]
            done = hidden.at[pl.ds(i * BLOCK, BLOCK), pl.ds(h * GROUP * HEAD, GROUP * HEAD)]
            put(done, hidden_out.at[pl.ds(i * BLOCK, BLOCK), pl.ds(h * GROUP * HEAD, GROUP * HEAD)])

    for r in range(0, TOK, 16):
        part = hidden[r : r + 16, :]
        spread = jnp.mean(part * part, axis=1, keepdims=True)
        normed[r : r + 16, :] = (part * lax.rsqrt(spread + 1e-6) * gain[...]).astype(BF16)

    put(normed, normed_out)
    for copy in puts:
        copy.wait()


def front(con, near, bias, q, fk, fv, res, gain, routes, gates):
    part = (HEADS_KV, SLOTS * BLOCK, HEAD)
    hbm = pl.BlockSpec(memory_space=pltpu.HBM)
    args = (con, near, routes.T, gates.T, q, bias, fk, fv, res, gain.reshape(1, D))
    shapes = [((TOK, D), F32), ((TOK, D), BF16), ((TYPES, 4, 2, PLANE, TOK), BF16)]
    return pl.pallas_call(
        front_kernel,
        name="exchange_and_attention",
        out_shape=[jax.ShapeDtypeStruct(*one) for one in shapes],
        in_specs=[hbm] * len(args),
        out_specs=[hbm] * 3,
        scratch_shapes=[pltpu.VMEM(one.shape, one.dtype) for one in args]
        + [pltpu.VMEM(*one) for one in shapes]
        + [pltpu.VMEM((2,) + part, BF16)]
        + [pltpu.VMEM(part, BF16)] * 5
        + [
            pltpu.SemaphoreType.DMA((len(args),)),
            pltpu.SemaphoreType.DMA((6,)),
            pltpu.SemaphoreType.DMA((6,)),
            pltpu.SemaphoreType.DMA((6,)),
        ],
        compiler_params=pltpu.CompilerParams(
            collective_id=1, has_side_effects=True, vmem_limit_bytes=60 * 2**20
        ),
    )(*args)


def table_rows():
    row = lax.broadcasted_iota(jnp.int32, (MSG, TOK), 0)
    block = jnp.zeros((MSG, TOK), jnp.int32)
    for b in range(1, 8):
        block = block + jnp.where(row >= b * CAP, 1, 0)
    return block, (row - block * CAP).astype(F32)


def dispatch_kernel(
    normed_hbm, table_hbm, w_gate, w_up, act, tables_out,
    normed, table, x_all, tables, select, stage, got, weights, acc, swap, turn, sorted_rows,
    in_sem, w_sem, tab_s, tab_r, col_s, col_r, msg_s, msg_r,
):
    loads = [
        pltpu.make_async_copy(table_hbm, table, in_sem.at[0]),
        pltpu.make_async_copy(normed_hbm, normed, in_sem.at[1]),
    ]
    for load in loads:
        load.start()

    def weight_loads(j):
        return [
            pltpu.make_async_copy(
                w.at[pl.ds(pl.multiple_of(half * HALF + j * PIECE, PIECE), PIECE)],
                weights.at[j % 2, n, half],
                w_sem.at[j % 2, n, half],
            )
            for n, w in enumerate((w_gate, w_up))
            for half in range(2)
        ]

    for j in range(2):
        for load in weight_loads(j):
            load.start()
    greet_all()
    for load in loads:
        load.wait()

    def table_copy(n, t, dev, slot):
        return pltpu.make_async_remote_copy(
            src_ref=table.at[t, dev[2]], dst_ref=tables.at[t, slot], send_sem=tab_s.at[t, n], recv_sem=tab_r.at[t, n],
            device_id=turned_device(t, dev), device_id_type=MESH,
        )

    def column_copy(n, j, t, dev, slot):
        start = pl.multiple_of(dev[3] * HALF + j * PIECE, PIECE)
        return pltpu.make_async_remote_copy(
            src_ref=normed.at[:, pl.ds(start, PIECE)],
            dst_ref=x_all.at[j, pl.ds(pl.multiple_of(slot * TOK, TOK), TOK)],
            send_sem=col_s.at[j, n], recv_sem=col_r.at[j, n],
            device_id=turned_device(t, dev), device_id_type=MESH,
        )

    def send_tables(t):
        here = turned(t)
        me = here[2] * 2 + here[3]
        for n, o in enumerate(COLUMN):
            table_copy(n, t, to_column(o, here), me).start()
        tables[t, me] = table[t, here[2]]

    def await_tables(t):
        here = turned(t)
        for n, o in enumerate(COLUMN):
            dev = from_column(o, here)
            table_copy(n, t, dev, dev[2] * 2 + dev[3]).wait()
        tables_out[t] = tables[t].astype(F32)

    def send_columns(j):
        t = j % 3
        here = turned(t)
        me = here[2] * 2 + here[3]
        for n, o in enumerate(COLUMN):
            column_copy(n, j, t, to_column(o, here), me).start()
        start = pl.multiple_of(here[3] * HALF + j * PIECE, PIECE)
        x_all[j, pl.ds(pl.multiple_of(me * TOK, TOK), TOK), :] = normed[:, pl.ds(start, PIECE)]

    send_tables(0)
    send_columns(0)
    for t in range(1, TYPES):
        send_tables(t)

    def send_rest(j, carry):
        send_columns(j)
        return carry

    lax.fori_loop(1, PIECES, send_rest, 0)
    await_tables(0)

    block, place = table_rows()

    def fill(t):
        def one(l, carry):
            for b in range(8):
                row = tables_out[t, b, 0, pl.ds(l, 1), :]
                hit = (row == place) & (block == b)
                select[t, pl.ds(pl.multiple_of(l * MSG, 16), MSG), b * TOK : (b + 1) * TOK] = jnp.where(
                    hit, 1.0, 0.0
                ).astype(BF16)
            return carry

        lax.fori_loop(0, PLANE, one, 0)

    fill(0)

    def message(k, j, t, dev, src_dev):
        chip = src_dev[0] * 4 + src_dev[1]
        return pltpu.make_async_remote_copy(
            src_ref=stage.at[j % STAGED, pl.ds(pl.multiple_of(plane_index(dev) * MSG, 16), MSG)],
            dst_ref=got.at[j, src_dev[3], pl.ds(pl.multiple_of(chip * MSG, 16), MSG)],
            send_sem=msg_s.at[j, k], recv_sem=msg_r.at[j, k],
            device_id=turned_device(t, dev), device_id_type=MESH,
        )

    def sent(j):
        here = turned(j % 3)
        for k, o in enumerate(OFFSETS):
            message(k, j, j % 3, to_plane(o, here), here).wait_send()

    def send_piece(j):
        t = j % 3
        here = turned(t)
        for n, o in enumerate(COLUMN):
            dev = from_column(o, here)
            column_copy(n, j, t, dev, dev[2] * 2 + dev[3]).wait_recv()

        @pl.when(j >= STAGED)
        def _():
            sent(j - STAGED)

        step = ALL // 8

        def tile(i, carry):
            rows = pl.ds(pl.multiple_of(i * step, 16), step)
            stage[j % STAGED, rows, :] = jnp.dot(select[t, rows, :], x_all[j], preferred_element_type=F32).astype(BF16)
            return carry

        lax.fori_loop(0, 8, tile, 0)
        own_rows = pl.ds(pl.multiple_of(plane_index(here) * MSG, 16), MSG)
        own_place = pl.ds(pl.multiple_of((here[0] * 4 + here[1]) * MSG, 16), MSG)
        got[j, here[3], own_place, :] = stage[j % STAGED, own_rows, :]

    def start(k, j, t, here):
        message(k, j, t, to_plane(OFFSETS[k], here), here).start()

    def use_piece(j):
        t = j % 3
        here = turned(t)
        for load in weight_loads(j):
            load.wait()
        for k, o in enumerate(OFFSETS):
            message(k, j, t, here, from_plane(o, here)).wait_recv()

        @pl.when(t == 0)
        def _():
            sorted_rows[...] = got[j]

        @pl.when(t == 1)
        def _():
            for half in range(2):
                for i in range(4):
                    rows = slice(i * 320, (i + 1) * 320)
                    sorted_rows[half, rows, :] = jnp.dot(
                        swap[...], got[j, half, rows, :], preferred_element_type=F32
                    ).astype(BF16)

        @pl.when(t == 2)
        def _():
            def tile(i, carry):
                rows = pl.ds(pl.multiple_of(i * 320, 16), 320)
                turn[...] = turn_matrix(320, i * 320, False)
                for half in range(2):
                    sorted_rows[half, rows, :] = jnp.dot(
                        turn[...], got[j, half], preferred_element_type=F32
                    ).astype(BF16)
                return carry

            lax.fori_loop(0, 4, tile, 0)

        step = ROWS // 5

        def tile(i, carry):
            rows = pl.ds(pl.multiple_of(i * step, 16), step)
            left = sorted_rows[0, rows, :]
            right = sorted_rows[1, rows, :]
            for n in range(2):
                acc[n, rows, :] += jnp.dot(left, weights[j % 2, n, 0], preferred_element_type=F32) + jnp.dot(
                    right, weights[j % 2, n, 1], preferred_element_type=F32
                )
            return carry

        lax.fori_loop(0, 5, tile, 0)

        @pl.when(j + 2 < PIECES)
        def _():
            for load in weight_loads(j + 2):
                load.start()

    def step(j, carry):
        @pl.when(j < PIECES)
        def _():
            send_piece(j)

        roll(start, j)

        @pl.when(j == 0)
        def _():
            for t in range(1, TYPES):
                await_tables(t)
            acc[...] = jnp.zeros_like(acc)
            swap[...] = swap_matrix()

        @pl.when(j < 2)
        def _():
            fill(j + 1)

        @pl.when(j >= AHEAD)
        def _():
            use_piece(j - AHEAD)

        return carry

    lax.fori_loop(0, PIECES + AHEAD, step, 0)

    def finish(i, carry):
        rows = pl.ds(pl.multiple_of(i * MSG, 16), MSG)
        g = acc[0, rows, :]
        act[rows, :] = (g / (1.0 + jnp.exp(-g)) * acc[1, rows, :]).astype(BF16)
        return carry

    lax.fori_loop(0, ROWS // MSG, finish, 0)

    for j in range(PIECES - STAGED, PIECES):
        sent(j)

    def sent_columns(j, carry):
        here = turned(j % 3)
        for n, o in enumerate(COLUMN):
            column_copy(n, j, j % 3, to_column(o, here), here[2] * 2 + here[3]).wait_send()
        return carry

    lax.fori_loop(0, PIECES, sent_columns, 0)


def dispatch(normed, table, w_gate, w_up):
    vmem = pl.BlockSpec(memory_space=pltpu.VMEM)
    hbm = pl.BlockSpec(memory_space=pltpu.HBM)
    dma = pltpu.SemaphoreType.DMA
    return pl.pallas_call(
        dispatch_kernel,
        name="dispatch",
        out_shape=[
            jax.ShapeDtypeStruct((ROWS, FF), BF16),
            jax.ShapeDtypeStruct((TYPES, 8, 2, PLANE, TOK), F32),
        ],
        in_specs=[hbm] * 4,
        out_specs=[vmem] * 2,
        scratch_shapes=[
            pltpu.VMEM((TOK, D), BF16),
            pltpu.VMEM((TYPES, 4, 2, PLANE, TOK), BF16),
            pltpu.VMEM((PIECES, 8 * TOK, PIECE), BF16),
            pltpu.VMEM((TYPES, 8, 2, PLANE, TOK), BF16),
            pltpu.VMEM((TYPES, ALL, 8 * TOK), BF16),
            pltpu.VMEM((STAGED, ALL, PIECE), BF16),
            pltpu.VMEM((PIECES, 2, ROWS, PIECE), BF16),
            pltpu.VMEM((2, 2, 2, PIECE, FF), BF16),
            pltpu.VMEM((2, ROWS, FF), F32),
            pltpu.VMEM((320, 320), BF16),
            pltpu.VMEM((320, ROWS), BF16),
            pltpu.VMEM((2, ROWS, PIECE), BF16),
            dma((2,)),
            dma((2, 2, 2)),
            dma((TYPES, len(COLUMN))),
            dma((TYPES, len(COLUMN))),
            dma((PIECES, len(COLUMN))),
            dma((PIECES, len(COLUMN))),
            dma((PIECES, len(OFFSETS))),
            dma((PIECES, len(OFFSETS))),
        ],
        compiler_params=pltpu.CompilerParams(
            collective_id=2, has_side_effects=True, vmem_limit_bytes=62 * 2**20
        ),
    )(normed, table, w_gate, w_up)


def combine_kernel(
    act_hbm, tables_hbm, w_down, hidden_hbm, out,
    acts, tables, wd, hidden, answers, got, mix, partial, sums, swap, turn,
    in_sem, msg_s, msg_r, col_s, col_r,
):
    loads = [
        pltpu.make_async_copy(act_hbm, acts.at[0], in_sem.at[0]),
        pltpu.make_async_copy(w_down, wd, in_sem.at[1]),
        pltpu.make_async_copy(tables_hbm, tables, in_sem.at[2]),
        pltpu.make_async_copy(hidden_hbm, hidden, in_sem.at[3]),
    ]
    for load in loads:
        load.start()
    greet_all()
    for load in loads[:2]:
        load.wait()

    def message(k, j, t, dev, src_dev):
        chip = dev[0] * 4 + dev[1]
        return pltpu.make_async_remote_copy(
            src_ref=answers.at[j % ANSWERED, dev[3], pl.ds(pl.multiple_of(chip * MSG, 16), MSG)],
            dst_ref=got.at[j, pl.ds(pl.multiple_of(plane_index(src_dev) * MSG, 16), MSG)],
            send_sem=msg_s.at[j, k], recv_sem=msg_r.at[j, k],
            device_id=turned_device(t, dev), device_id_type=MESH,
        )

    def column_copy(n, j, t, dev, src_dev):
        block = dev[2] * 2 + dev[3]
        return pltpu.make_async_remote_copy(
            src_ref=partial.at[j, pl.ds(pl.multiple_of(block * TOK, TOK), TOK)],
            dst_ref=sums.at[j, src_dev[2], src_dev[3]],
            send_sem=col_s.at[j, n], recv_sem=col_r.at[j, n],
            device_id=turned_device(t, dev), device_id_type=MESH,
        )

    def sent(j):
        here = turned(j % 3)
        for k, o in enumerate(OFFSETS):
            message(k, j, j % 3, to_plane(o, here), here).wait_send()

    def sent_columns(j):
        here = turned(j % 3)
        for n, o in enumerate(COLUMN):
            column_copy(n, j, j % 3, to_column(o, here), here).wait_send()

    def send_piece(j):
        t = j % 3
        here = turned(t)
        for half in range(2):
            span = pl.ds(pl.multiple_of(half * HALF + j * PIECE, PIECE), PIECE)

            def tile(i, inner):
                rows = pl.ds(pl.multiple_of(i * (ROWS // 4), 16), ROWS // 4)
                answers[j % ANSWERED, half, rows, :] = jnp.dot(
                    acts[t, rows, :], wd[:, span], preferred_element_type=F32
                ).astype(BF16)
                return inner

            lax.fori_loop(0, 4, tile, 0)
        own_rows = pl.ds(pl.multiple_of(plane_index(here) * MSG, 16), MSG)
        own_place = pl.ds(pl.multiple_of((here[0] * 4 + here[1]) * MSG, 16), MSG)
        got[j, own_rows, :] = answers[j % ANSWERED, here[3], own_place, :]
        for k, o in enumerate(OFFSETS):
            message(k, j, t, to_plane(o, here), here).start()

    send_piece(0)
    swap[...] = swap_matrix()
    for i in range(4):
        rows = slice(i * 320, (i + 1) * 320)
        acts[1, rows, :] = jnp.dot(swap[...], acts[0, rows, :], preferred_element_type=F32).astype(BF16)
    send_piece(1)

    def turn_rows(i, carry):
        turn[...] = turn_matrix(64, i * 64, True)
        acts[2, pl.ds(pl.multiple_of(i * 64, 64), 64), :] = jnp.dot(
            turn[...], acts[0], preferred_element_type=F32
        ).astype(BF16)
        return carry

    lax.fori_loop(0, ROWS // 64, turn_rows, 0)

    def send_more(j, carry):
        send_piece(j)
        return carry

    lax.fori_loop(2, ANSWERED, send_more, 0)

    for load in loads[2:]:
        load.wait()
    block, place = table_rows()

    def fill(i, carry):
        t = i // 4
        p = i % 4
        for b in range(8):
            rows = []
            for n in range(8):
                l = p * 8 + n
                hit = (tables[t, b, 0, pl.ds(l, 1), :] == place) & (block == b)
                rows.append(jnp.where(hit, tables[t, b, 1, pl.ds(l, 1), :], 0.0))
            whole = jnp.concatenate(rows, axis=0)
            mix[t, b * TOK : (b + 1) * TOK, pl.ds(pl.multiple_of(p * 8 * MSG, TOK), 8 * MSG)] = whole.T.astype(BF16)
        return carry

    lax.fori_loop(0, TYPES * PLANE // 8, fill, 0)

    def reduce_piece(j):
        t = j % 3
        here = turned(t)
        for k, o in enumerate(OFFSETS):
            message(k, j, t, here, from_plane(o, here)).wait_recv()

        for far in (2, 1, 3, 0):
            rows = pl.ds(pl.multiple_of(((here[2] + far) % 4) * 2 * TOK, 2 * TOK), 2 * TOK)
            partial[j, rows, :] = jnp.dot(mix[t, rows, :], got[j], preferred_element_type=F32).astype(BF16)
            for n, o in enumerate(COLUMN):
                if o[0] == far:
                    column_copy(n, j, t, to_column(o, here), here).start()
        me = here[2] * 2 + here[3]
        sums[j, here[2], here[3]] = partial[j, pl.ds(pl.multiple_of(me * TOK, TOK), TOK), :]

    def finish_piece(j):
        t = j % 3
        here = turned(t)
        for n, o in enumerate(COLUMN):
            column_copy(n, j, t, here, from_column(o, here)).wait_recv()
        for half in range(2):
            span = pl.ds(pl.multiple_of(half * HALF + j * PIECE, PIECE), PIECE)
            total = hidden[:, span]
            for n in range(4):
                total = total + sums[j, n, half].astype(F32)
            out[:, span] = total.astype(BF16)

    def step(j, carry):
        @pl.when(j < PIECES)
        def _():
            reduce_piece(j)

        @pl.when(j < PIECES - ANSWERED)
        def _():
            sent(j)
            send_piece(j + ANSWERED)

        @pl.when(j >= BEHIND)
        def _():
            finish_piece(j - BEHIND)

        return carry

    lax.fori_loop(0, PIECES + BEHIND, step, 0)

    for j in range(PIECES - ANSWERED, PIECES):
        sent(j)
    for j in range(PIECES):
        sent_columns(j)


def combine(act, tables, w_down, hidden):
    hbm = pl.BlockSpec(memory_space=pltpu.HBM)
    dma = pltpu.SemaphoreType.DMA
    return pl.pallas_call(
        combine_kernel,
        name="combine",
        out_shape=jax.ShapeDtypeStruct((TOK, D), BF16),
        in_specs=[hbm] * 4,
        out_specs=pl.BlockSpec(memory_space=pltpu.VMEM),
        scratch_shapes=[
            pltpu.VMEM((TYPES, ROWS, FF), BF16),
            pltpu.VMEM((TYPES, 8, 2, PLANE, TOK), F32),
            pltpu.VMEM((FF, D), BF16),
            pltpu.VMEM((TOK, D), F32),
            pltpu.VMEM((ANSWERED, 2, ROWS, PIECE), BF16),
            pltpu.VMEM((PIECES, ALL, PIECE), BF16),
            pltpu.VMEM((TYPES, 8 * TOK, ALL), BF16),
            pltpu.VMEM((PIECES, 8 * TOK, PIECE), BF16),
            pltpu.VMEM((PIECES, 4, 2, TOK, PIECE), BF16),
            pltpu.VMEM((320, 320), BF16),
            pltpu.VMEM((64, ROWS), BF16),
            dma((4,)),
            dma((PIECES, len(OFFSETS))),
            dma((PIECES, len(OFFSETS))),
            dma((PIECES, len(COLUMN))),
            dma((PIECES, len(COLUMN))),
        ],
        compiler_params=pltpu.CompilerParams(
            collective_id=3, has_side_effects=True, vmem_limit_bytes=62 * 2**20
        ),
    )(act, tables, w_down, hidden)


def body(
    queries, fresh_keys, fresh_values, stored_keys, stored_values, column_blocks, diagonal_offsets,
    residual, norm_gain, routes, gate_weights, w_gate, w_up, w_down,
):
    con, near, bias = collect(column_blocks, diagonal_offsets, stored_keys, stored_values)
    hidden, normed, table = front(
        con, near, bias, queries, fresh_keys, fresh_values, residual, norm_gain, routes, gate_weights
    )
    act, tables = dispatch(normed, table, w_gate[0], w_up[0])
    return combine(act, tables, w_down[0], hidden)


def solution(mesh):
    rows = P(("ctx", "exp"), None)
    experts = P(("ctx", "exp"), None, None)
    in_specs = (
        rows, rows, rows, P("ctx", None), P("ctx", None), P(), P(), rows, P(), rows, rows,
        experts, experts, experts,
    )
    return jax.shard_map(body, mesh=mesh, in_specs=in_specs, out_specs=rows, check_vma=False)
```
